32 devices in a mesh: chan: 16 (over z, y, x), tm: 2 (over core).
Axes of the slice: x: 2, y: 2, z: 4, core: 2. Of those that a mesh axis runs over, the one named last changes fastest.
Arguments:
- signal: bfloat16 [1280, 16384], P('chan', 'tm'), may hold values from -6 to 6
- channel_mask: int32 [1280], P('chan'), may hold values 0 or 1
- seg_offsets: int32 [256], P('tm'), may hold values from 0 to 8191, as said below
- slow_steps: int32 [512], replicated, may hold values from -512 to 512
Outputs:
- beam: float32 [128, 2, 512, 256], P('chan', None, None, 'tm')
- power: float32 [512, 256], P('chan', 'tm')
The draws below stay inside these ranges and needn't reach their ends.
Inputs may be any that keep to these rules, and one draw needn't show every extreme that they name: `seg_offsets`: entry s lies in [(s mod 128) * 64, (s mod 128) * 64 + 63]; some entry reaches the top of its interval.
All inputs are finite; a program needn't handle non-finite values. No bound on the sum of `channel_mask` on one device may be relied on, other than what follows from the above.
Results may differ from the reference program's by a relative error of at most 0.0048.
Values may be sent and summed in bfloat16 or wider, within the bound.
A program may use at most 64 MiB of HBM per device.

```python
import math
import jax
import jax.numpy as jnp
from jax import lax

T_DEV = 8192
SEG = 256
NF = 128
NP = 512
SUBSTEPS = 16
MAXSTEP = 512
HOP = 64
NSEG_DEV = 128
NC = 1280
NT = 16384
NSEG = 256
N_TM = 2


def draw_seg_offsets(key, part):
    jitter = jax.random.randint(jax.random.fold_in(key, 11), (NSEG,), 0, HOP)
    picked = jax.random.randint(jax.random.fold_in(key, 12), (), 0, NSEG // NSEG_DEV)
    topmost = picked * NSEG_DEV + NSEG_DEV - 1
    places = jnp.arange(NSEG, dtype=jnp.int32)
    jitter = jnp.where(places == topmost, HOP - 1, jitter)
    local = places % NSEG_DEV
    return (local * HOP + jitter).astype(jnp.int32)


def with_ends(result, stream_key, smallest, high):
    shape = result.shape
    index_at = [jax.random.randint(jax.random.fold_in(stream_key, axis), (), 0, shape[axis]) for axis in range(len(shape))]
    result = result.at[tuple(index_at)].set(smallest)
    longest = shape.index(max(shape))
    index_at[longest] = (index_at[longest] + 1) % shape[longest]
    return result.at[tuple(index_at)].set(high)


def shard_levels(stream_key, shape, split, least, high):
    loudness, own = 1.0, jax.random.fold_in(stream_key, 6)
    for dim, shards_of in split:
        draws = jnp.exp(jax.random.uniform(jax.random.fold_in(own, dim), (shards_of,), jnp.float32, least / len(split), high / len(split)))
        loudness = loudness * jnp.repeat(draws, shape[dim] // shards_of).reshape([-1 if axis == dim else 1 for axis in range(len(shape))])
    return loudness


def normal_values(own_key, shape, deviation, limit, cuts=(), kind=jnp.bfloat16):
    factor_of = shard_levels(own_key, shape, cuts, -0.22, 0.18) if cuts else 1.0
    values = jax.random.normal(own_key, shape, jnp.float32) * deviation * factor_of
    return jnp.minimum(jnp.maximum(values, -limit), limit).astype(kind)


def setup_inputs(seed: int = 0) -> dict:
    splits = jax.random.split(jax.random.key(seed), 5)
    return {
        "signal": normal_values(splits[0], (NC, NT), 1.0, 6.0, ((0, 16), (1, 2))),
        "channel_mask": with_ends((jax.random.randint(splits[1], (NC,), 0, 16) < 15).astype(jnp.int32), jax.random.fold_in(splits[1], 1), 0, 1),
        "seg_offsets": draw_seg_offsets(jax.random.fold_in(splits[4], 71), 0),
        "slow_steps": with_ends(jax.random.randint(splits[3], (NP,), 0 - MAXSTEP, MAXSTEP + 1), jax.random.fold_in(splits[3], 1), 0 - MAXSTEP, MAXSTEP).astype(jnp.int32),
    }


def make_table():
    points = jnp.arange(SEG, dtype=jnp.int32)
    bins = jnp.arange(1, NF + 1, dtype=jnp.int32)
    taper = 0.5 - 0.5 * jnp.cos(2.0 * jnp.pi * points.astype(jnp.float32) / SEG)
    index = jnp.mod(bins[:, None] * points[None, :], SEG)
    angle = index.astype(jnp.float32) * (2.0 * jnp.pi / SEG)
    scale = 1.0 / math.sqrt(3.0 * SEG / 8.0)
    table = jnp.stack([taper * jnp.cos(angle), -taper * jnp.sin(angle)], axis=1) * scale
    return table.astype(jnp.bfloat16)

def steering(bins, slow_steps, chans, total):
    modulus = SEG * SUBSTEPS
    product = jnp.mod(bins[:, None] * slow_steps[None, :], modulus)
    index = jnp.mod(product[:, :, None] * chans[None, None, :], modulus)
    theta = index.astype(jnp.float32) * (2.0 * jnp.pi / modulus)
    scale = 1.0 / math.sqrt(total)
    return (jnp.stack([jnp.cos(theta), jnp.sin(theta)], axis=1) * scale).astype(jnp.bfloat16)

def reference(signal, channel_mask, seg_offsets, slow_steps):
    table = make_table().astype(jnp.float32)
    masked = signal * channel_mask[:, None].astype(jnp.bfloat16)
    padded = jnp.concatenate([masked, jnp.zeros((NC, SEG), jnp.bfloat16)], axis=1)
    bins = jnp.arange(1, NF + 1, dtype=jnp.int32)
    chans = jnp.arange(NC, dtype=jnp.int32)
    offsets = seg_offsets.reshape(N_TM, NSEG_DEV)
    window = jnp.arange(SEG, dtype=jnp.int32)

    def one_block(block):
        starts = (block * T_DEV + offsets[block]).astype(jnp.int32)
        columns = starts[:, None] + window[None, :]
        pieces = padded[:, columns].astype(jnp.float32)
        spectra = jnp.einsum('fpn,csn->fcps', table, pieces).astype(jnp.bfloat16)

        def one_bin(freq):
            steer = steering(bins[freq][None], slow_steps, chans, NC)[0].astype(jnp.float32)
            spec = spectra[freq].astype(jnp.float32)
            prod = jnp.einsum('apc,cbs->apbs', steer, spec)
            real = prod[0, :, 0] - prod[1, :, 1]
            imag = prod[0, :, 1] + prod[1, :, 0]
            return jnp.stack([real, imag])
        return lax.map(one_bin, jnp.arange(NF, dtype=jnp.int32))
    beams = lax.map(one_block, jnp.arange(N_TM, dtype=jnp.int32))
    beam = jnp.transpose(beams, (1, 2, 3, 0, 4)).reshape(NF, 2, NP, NSEG)
    power = lax.optimization_barrier(jnp.sum(beam[:, 0] * beam[:, 0] + beam[:, 1] * beam[:, 1], axis=0)) / NF
    return (beam, power)
```

```python
import functools
import math

import jax
import jax.numpy as jnp
import ml_dtypes
import numpy as np
from jax import lax
from jax.experimental import pallas as pl
from jax.experimental.pallas import tpu as pltpu
from jax.sharding import PartitionSpec as P

SEG = 256
NF = 128
NP = 512
SUBSTEPS = 16
HOP = 64
LANES = 128
CHUNK = 16
ROWS = 64
VMEM_LIMIT = 46 * 1024 * 1024


def make_table():
    points = np.arange(SEG)
    bins = np.arange(1, NF + 1)
    taper = 0.5 - 0.5 * np.cos(2.0 * np.pi * points / SEG)
    angle = ((bins[:, None] * points[None, :]) % SEG) * (2.0 * np.pi / SEG)
    scale = 1.0 / math.sqrt(3.0 * SEG / 8.0)
    table = np.stack([taper * np.cos(angle), -taper * np.sin(angle)]).reshape(2, 2, NF // 2, SEG) * scale
    table = table.transpose(1, 0, 2, 3).reshape(2 * NF, SEG)
    return jnp.asarray(table.astype(np.float32).astype(ml_dtypes.bfloat16))


def turn(index):
    quarter = SEG * SUBSTEPS // 4
    quadrant = (index + quarter // 2) >> 10
    x = (index - quadrant * quarter).astype(jnp.float32) * (0.5 * math.pi / quarter)
    y = x * x
    sin = x * (1.0 + y * (-1.0 / 6 + y * (1.0 / 120 + y * (-1.0 / 5040 + y * (1.0 / 362880)))))
    cos = 1.0 + y * (-0.5 + y * (1.0 / 24 + y * (-1.0 / 720 + y * (1.0 / 40320))))
    odd = (quadrant & 1) == 1
    c, d = jnp.where(odd, sin, cos), jnp.where(odd, cos, sin)
    return jnp.where(((quadrant + 1) & 2) == 2, -c, c), jnp.where((quadrant & 2) == 2, -d, d)


def fused_kernel(offs, x_ref, mask_ref, table_ref, slow_ref, beam_ref, power_ref, slow, held_signal, p0, p1, s0, s1, send, recv, steer, terms, arrived, send_sems, recv_sems, power_sems, halo_sems, signal_sends, signal_recvs, *, ranks, blocks):
    chans = x_ref.shape[0]
    chunks = chans // CHUNK
    segs = p0.shape[0] // CHUNK
    own = NF // ranks
    slows = NP // ranks
    width = ranks * CHUNK
    total = chans * ranks
    modulus = SEG * SUBSTEPS
    me = lax.axis_index("chan")

    tm = lax.axis_index("tm")
    half = ranks // 2
    side = me // half
    mirror = (1 - side) * half + lax.rem(me, half)
    span = x_ref.shape[1]
    half_bins = NF // 2

    def peer(d):
        return (1 - side + d // half) % 2 * half + ((me % half) ^ (d % half))

    barrier = pltpu.get_barrier_semaphore()
    mesh_ids = pl.DeviceIdType.MESH

    def greet(d, carry):
        pl.semaphore_signal(barrier, inc=1, device_id={"chan": peer(d)}, device_id_type=mesh_ids)
        return carry

    def others_of(body):
        lax.fori_loop(0, half, body, 0)
        lax.fori_loop(half + 1, ranks, body, 0)

    @pl.when(tm > 0)
    def _():
        pl.semaphore_signal(barrier, inc=1, device_id={"tm": tm - 1}, device_id_type=mesh_ids)

    @pl.when(tm < blocks - 1)
    def _():
        pl.semaphore_signal(barrier, inc=1, device_id={"tm": tm + 1}, device_id_type=mesh_ids)

    others_of(greet)

    def mask_rows(chunk, carry):
        rows = pl.ds(pl.multiple_of(chunk * CHUNK, CHUNK), CHUNK)
        across = lax.broadcasted_iota(jnp.int32, (CHUNK, chans), 1)
        down = lax.broadcasted_iota(jnp.int32, (CHUNK, chans), 0) + chunk * CHUNK
        live = jnp.broadcast_to(mask_ref[...].astype(jnp.float32), (CHUNK, chans))
        mask = jnp.sum(jnp.where(across == down, live, 0.0), axis=1, keepdims=True)
        mask = jnp.broadcast_to(mask, (CHUNK, LANES))

        def one(tile, carry):
            columns = pl.ds(pl.multiple_of(tile * LANES, LANES), LANES)
            held_signal[0, rows, columns] = (x_ref[rows, columns].astype(jnp.float32) * mask).astype(jnp.bfloat16)
            return carry

        return lax.fori_loop(0, span // LANES, one, carry, unroll=8)

    lax.fori_loop(0, chunks, mask_rows, 0)
    pl.semaphore_wait(barrier, ranks - 1 + jnp.where(tm > 0, 1, 0) + jnp.where(tm < blocks - 1, 1, 0))

    def halo_copy(to):
        return pltpu.make_async_remote_copy(
            src_ref=held_signal.at[0, :, pl.ds(0, SEG)],
            dst_ref=held_signal.at[0, :, pl.ds(span, SEG)],
            send_sem=halo_sems.at[0],
            recv_sem=halo_sems.at[1],
            device_id={"tm": to},
            device_id_type=mesh_ids,
        )

    def mirror_copy(rows, columns, send_sem, recv_sem):
        return pltpu.make_async_remote_copy(
            src_ref=held_signal.at[0, rows, columns],
            dst_ref=held_signal.at[1, rows, columns],
            send_sem=send_sem,
            recv_sem=recv_sem,
            device_id={"chan": mirror},
            device_id_type=mesh_ids,
        )

    def signal_copy(chunk):
        rows = pl.ds(pl.multiple_of(chunk * CHUNK, CHUNK), CHUNK)
        return mirror_copy(rows, pl.ds(0, span), signal_sends.at[chunk], signal_recvs.at[chunk])

    relay = mirror_copy(pl.ds(0, chans), pl.ds(span, SEG), halo_sems.at[2], halo_sems.at[3])

    @pl.when(tm > 0)
    def _():
        halo_copy(tm - 1).start()

    def send_signal(chunk, carry):
        signal_copy(chunk).start()
        return carry

    lax.fori_loop(0, 2, send_signal, 0)

    @pl.when(tm == blocks - 1)
    def _():
        held_signal[0, :, span:] = jnp.zeros((chans, SEG), jnp.bfloat16)

    for block in range(NP // LANES):
        row = slow_ref[:, block * LANES:(block + 1) * LANES].astype(jnp.float32)
        across = lax.broadcasted_iota(jnp.int32, (LANES, LANES), 1)
        down = lax.broadcasted_iota(jnp.int32, (LANES, LANES), 0)
        column = jnp.sum(jnp.where(across == down, jnp.broadcast_to(row, (LANES, LANES)), 0.0), axis=1, keepdims=True)
        slow[block * LANES:(block + 1) * LANES, :] = jnp.broadcast_to(column, (LANES, LANES)).astype(jnp.int32)

    @pl.when(tm < blocks - 1)
    def _():
        halo_copy(tm + 1).wait_recv()

    relay.start()

    def block_copy(slot, chunk, origin, to):
        return pltpu.make_async_remote_copy(
            src_ref=send.at[slot, chunk, pl.ds(lax.rem(to, half) * own, own)],
            dst_ref=recv.at[chunk, origin],
            send_sem=send_sems.at[slot, chunk],
            recv_sem=recv_sems.at[chunk],
            device_id={"chan": to},
            device_id_type=mesh_ids,
        )

    def spectra(slot, chunk, origin):
        top = pl.multiple_of(chunk * CHUNK, CHUNK)

        def gather(s, carry):
            start = pl.multiple_of((s // 2) * LANES, LANES)
            back = LANES - (offs[s] - start)
            tiles = held_signal[slot, pl.ds(top, CHUNK), pl.ds(start, 3 * LANES)].astype(jnp.float32)
            a, b, c = [pltpu.roll(tiles[:, i * LANES:(i + 1) * LANES], back, 1) for i in range(3)]
            keep = lax.broadcasted_iota(jnp.int32, (CHUNK, LANES), 1) < back
            p0[pl.ds(s, CHUNK, stride=segs), :] = jnp.where(keep, a, b)
            p1[pl.ds(s, CHUNK, stride=segs), :] = jnp.where(keep, b, c)
            return carry

        lax.fori_loop(0, segs, gather, 0, unroll=16)
        table = table_ref[pl.ds(pl.multiple_of(side * NF, NF), NF), :]

        def transform(i, carry):
            rows = pl.ds(pl.multiple_of(i * 2 * segs, 2 * segs), 2 * segs)
            piece = jnp.concatenate([p0[rows, :], p1[rows, :]], axis=1).astype(jnp.bfloat16)
            spec = lax.dot_general(table, piece, (((1,), (1,)), ((), ())), preferred_element_type=jnp.float32)
            for part in range(2):
                both = spec[:, part * segs:(part + 1) * segs]
                s0[pl.ds(2 * i + part, half_bins, stride=CHUNK), :] = both[:half_bins]
                s1[pl.ds(2 * i + part, half_bins, stride=CHUNK), :] = both[half_bins:]
            return carry

        lax.fori_loop(0, CHUNK // 2, transform, 0, unroll=8)

        def pack(f, carry):
            rows = pl.ds(pl.multiple_of(f * CHUNK, CHUNK), CHUNK)
            send[slot, chunk, f] = jnp.concatenate([s0[rows, :], s1[rows, :]], axis=1).astype(jnp.bfloat16)
            return carry

        lax.fori_loop(0, half_bins, pack, 0, unroll=8)

        def launch(d, carry):
            block_copy(slot, chunk, origin, peer(ranks + half - d)).start()
            return carry

        lax.fori_loop(half + 1, ranks, launch, 0)
        recv[chunk, origin] = send[slot, chunk, pl.ds(lax.rem(me, half) * own, own)]

    def own_spectra(chunk, carry):
        spectra(0, chunk, me)
        return carry

    lax.fori_loop(0, chunks, own_spectra, 0)

    def steering(step, carry):
        f, rows = step // (NP // ROWS), lax.rem(step, NP // ROWS) * ROWS
        rows = pl.multiple_of(rows, ROWS)
        kp = (slow[pl.ds(rows, ROWS), :] * (me * own + f + 1)) & (modulus - 1)
        lane = lax.broadcasted_iota(jnp.int32, (ROWS, LANES), 1)
        first = (lane // CHUNK) * chans + (lane & (CHUNK - 1))
        scale = 1.0 / math.sqrt(total)
        cos0, sin0 = turn((kp * first) & (modulus - 1))
        cos0, sin0 = cos0 * scale, sin0 * scale
        hops = jnp.where(lane == 0, CHUNK, (LANES // CHUNK) * chans)
        cosp, sinp = turn((kp * hops) & (modulus - 1))
        rc, rs, bc, bs = [jnp.broadcast_to(v[:, i:i + 1], (ROWS, LANES)) for i in (0, 1) for v in (cosp, sinp)]
        for block in range(width // LANES):
            columns = slice(block * LANES, (block + 1) * LANES)
            cos, sin = cos0, sin0
            for chunk in range(chunks):
                steer[f, chunk, pl.ds(rows, ROWS), columns] = cos.astype(jnp.bfloat16)
                steer[f, chunk, pl.ds(NP + rows, ROWS), columns] = sin.astype(jnp.bfloat16)
                cos, sin = cos * rc - sin * rs, cos * rs + sin * rc
            cos0, sin0 = cos0 * bc - sin0 * bs, cos0 * bs + sin0 * bc
        return carry

    relay.wait_recv()
    steps = own * (NP // ROWS)

    def mirror_spectra(chunk, carry):
        lax.fori_loop(steps * chunk // (2 * chunks), steps * (chunk + 1) // (2 * chunks), steering, 0)
        signal_copy(chunk).wait_send()

        @pl.when(chunk + 2 < chunks)
        def _():
            signal_copy(chunk + 2).start()

        signal_copy(chunk).wait_recv()
        spectra(1, chunk, mirror)
        return carry

    lax.fori_loop(0, chunks, mirror_spectra, 0)
    lax.fori_loop(steps // 2, steps, steering, 0)

    others = pl.ds(0, ranks - 1)

    def add(chunk, first, last):
        held = recv.at[chunk, pl.ds(0, ranks - 2)]
        pltpu.make_async_copy(held, held, recv_sems.at[chunk]).wait()

        def one_bin(f, carry):
            spec = recv[chunk, :, f].reshape(width, 2 * segs)
            both = jnp.dot(steer[f, chunk], spec, preferred_element_type=jnp.float32)
            real = both[:NP, :segs] - both[NP:, segs:]
            imag = both[:NP, segs:] + both[NP:, :segs]
            beam_ref[f, 0] = real if first else beam_ref[f, 0] + real
            beam_ref[f, 1] = imag if first else beam_ref[f, 1] + imag
            return carry

        lax.fori_loop(0, own, one_bin, 0)

    add(0, True, False)

    def more(chunk, carry):
        add(chunk, False, False)
        return carry

    lax.fori_loop(1, chunks - 1, more, 0)
    add(chunks - 1, False, True)

    def power_copy(to):
        return pltpu.make_async_remote_copy(
            src_ref=terms.at[to],
            dst_ref=arrived.at[me],
            send_sem=power_sems.at[0],
            recv_sem=power_sems.at[1],
            device_id={"chan": to},
            device_id_type=pl.DeviceIdType.MESH,
        )

    def power_of(to):
        rows = pl.ds(pl.multiple_of(to * slows, slows), slows)

        def one_bin(f, acc):
            real, imag = beam_ref[f, 0, rows, :], beam_ref[f, 1, rows, :]
            return acc + (real * real + imag * imag)

        acc = lax.fori_loop(0, own, one_bin, jnp.zeros((slows, segs), jnp.float32), unroll=2)
        return acc * (1.0 / NF)

    def power_term(d, carry):
        to = peer(d)
        terms[to] = power_of(to).astype(terms.dtype)
        power_copy(to).start()
        return carry

    others_of(power_term)
    arrived[me] = power_of(me).astype(arrived.dtype)
    pltpu.make_async_copy(arrived.at[others], arrived.at[others], power_sems.at[1]).wait()

    def sum_up(r, acc):
        return acc + arrived[r].astype(jnp.float32)

    power_ref[...] = lax.fori_loop(0, ranks, sum_up, jnp.zeros((slows, segs), jnp.float32))

    def finish(chunk, carry):
        sent = recv.at[chunk, pl.ds(0, half - 1)]
        pltpu.make_async_copy(sent, sent, send_sems.at[0, chunk]).wait()
        pltpu.make_async_copy(sent, sent, send_sems.at[1, chunk]).wait()
        return carry

    lax.fori_loop(0, chunks, finish, 0)
    pltpu.make_async_copy(terms.at[others], terms.at[others], power_sems.at[0]).wait()

    relay.wait_send()

    @pl.when(tm > 0)
    def _():
        halo_copy(tm - 1).wait_send()


def fused(signal, mask, offsets, table, slow, ranks, blocks):
    chans, segs = signal.shape[0], offsets.shape[0]
    slows = NP // ranks
    term = jnp.bfloat16 if slows % 16 == 0 else jnp.float32
    own, chunks = NF // ranks, chans // CHUNK
    vmem = pl.BlockSpec(memory_space=pltpu.VMEM)
    return pl.pallas_call(
        functools.partial(fused_kernel, ranks=ranks, blocks=blocks),
        out_shape=(
            pltpu.VMEM((own, 2, NP, segs), jnp.float32),
            pltpu.VMEM((NP // ranks, segs), jnp.float32),
        ),
        in_specs=[pl.BlockSpec(memory_space=pltpu.SMEM), vmem, vmem, vmem, vmem],
        out_specs=(vmem, vmem),
        scratch_shapes=[
            pltpu.VMEM((NP, LANES), jnp.int32),
            pltpu.VMEM((2, chans, signal.shape[1] + SEG), jnp.bfloat16),
        ]
        + [pltpu.VMEM((CHUNK * segs, LANES), jnp.float32)] * 2
        + [pltpu.VMEM((NF // 2 * CHUNK, segs), jnp.float32)] * 2
        + [
            pltpu.VMEM((2, chunks, NF // 2, CHUNK, 2 * segs), jnp.bfloat16),
            pltpu.VMEM((chunks, ranks, own, CHUNK, 2 * segs), jnp.bfloat16),
            pltpu.VMEM((own, chunks, 2 * NP, ranks * CHUNK), jnp.bfloat16),
            pltpu.VMEM((ranks, slows, segs), term),
            pltpu.VMEM((ranks, slows, segs), term),
            pltpu.SemaphoreType.DMA((2, chunks)),
            pltpu.SemaphoreType.DMA((chunks,)),
            pltpu.SemaphoreType.DMA((2,)),
            pltpu.SemaphoreType.DMA((4,)),
            pltpu.SemaphoreType.DMA((chunks,)),
            pltpu.SemaphoreType.DMA((chunks,)),
        ],
        compiler_params=pltpu.CompilerParams(vmem_limit_bytes=VMEM_LIMIT, collective_id=0, has_side_effects=True),
        cost_estimate=pl.CostEstimate(flops=7 << 30, bytes_accessed=8 << 20, transcendentals=0),
        name="beamform",
    )(*[pltpu.with_memory_space_constraint(x, pltpu.HBM) for x in (offsets, signal, mask, table, slow)])


def local(signal, channel_mask, seg_offsets, slow_steps):
    ranks, blocks = lax.axis_size("chan"), lax.axis_size("tm")
    return fused(signal, channel_mask[None, :], seg_offsets, make_table(), slow_steps[None, :], ranks, blocks)


def solution(mesh):
    in_specs = (P("chan", "tm"), P("chan"), P("tm"), P())
    out_specs = (P("chan", None, None, "tm"), P("chan", "tm"))
    return jax.shard_map(local, mesh=mesh, in_specs=in_specs, out_specs=out_specs, check_vma=False)
```

```python
import functools
import math

import jax
import jax.numpy as jnp
import ml_dtypes
import numpy as np
from jax import lax
from jax.experimental import pallas as pl
from jax.experimental.pallas import tpu as pltpu
from jax.sharding import PartitionSpec as P

SEG = 256
NF = 128
NP = 512
SUBSTEPS = 16
HOP = 64
LANES = 128
CHUNK = 16
ROWS = 64
PAD = 8
VMEM_LIMIT = 46 * 1024 * 1024


def make_table():
    points = np.arange(SEG)
    bins = np.arange(1, NF + 1)
    taper = 0.5 - 0.5 * np.cos(2.0 * np.pi * points / SEG)
    angle = ((bins[:, None] * points[None, :]) % SEG) * (2.0 * np.pi / SEG)
    scale = 1.0 / math.sqrt(3.0 * SEG / 8.0)
    table = np.stack([taper * np.cos(angle), -taper * np.sin(angle)]).reshape(2, 2, NF // 2, SEG) * scale
    table = table.transpose(1, 0, 2, 3).reshape(2 * NF, SEG)
    return jnp.asarray(table.astype(np.float32).astype(ml_dtypes.bfloat16))


def turn(index):
    quarter = SEG * SUBSTEPS // 4
    quadrant = (index + quarter // 2) >> 10
    x = (index - quadrant * quarter).astype(jnp.float32) * (0.5 * math.pi / quarter)
    y = x * x
    sin = x * (1.0 + y * (-1.0 / 6 + y * (1.0 / 120 + y * (-1.0 / 5040 + y * (1.0 / 362880)))))
    cos = 1.0 + y * (-0.5 + y * (1.0 / 24 + y * (-1.0 / 720 + y * (1.0 / 40320))))
    odd = (quadrant & 1) == 1
    c, d = jnp.where(odd, sin, cos), jnp.where(odd, cos, sin)
    return jnp.where(((quadrant + 1) & 2) == 2, -c, c), jnp.where((quadrant & 2) == 2, -d, d)


def fused_kernel(offs, x_ref, mask_ref, table_ref, slow_ref, beam_ref, power_ref, slow, held_signal, p0, p1, s0, s1, send, recv, steer, energy, terms, arrived, send_sems, recv_sems, power_sems, halo_sems, signal_sends, signal_recvs, edge_sends, edge_recvs, *, ranks, blocks):
    chans = x_ref.shape[0]
    chunks = chans // CHUNK
    step = p0.shape[0] // CHUNK
    segs = step - PAD
    own = NF // ranks
    slows = NP // ranks
    width = ranks * CHUNK
    total = chans * ranks
    modulus = SEG * SUBSTEPS
    me = lax.axis_index("chan")

    tm = lax.axis_index("tm")
    half = ranks // 2
    side = me // half
    mirror = (1 - side) * half + lax.rem(me, half)
    span = x_ref.shape[1]
    half_bins = NF // 2

    def peer(d):
        return (1 - side + d // half) % 2 * half + ((me % half) ^ (d % half))

    barrier = pltpu.get_barrier_semaphore()
    mesh_ids = pl.DeviceIdType.MESH

    def greet(d, carry):
        pl.semaphore_signal(barrier, inc=1, device_id={"chan": peer(d)}, device_id_type=mesh_ids)
        return carry

    def others_of(body):
        lax.fori_loop(0, half, body, 0)
        lax.fori_loop(half + 1, ranks, body, 0)

    @pl.when(tm > 0)
    def _():
        pl.semaphore_signal(barrier, inc=1, device_id={"tm": tm - 1}, device_id_type=mesh_ids)

    @pl.when(tm < blocks - 1)
    def _():
        pl.semaphore_signal(barrier, inc=1, device_id={"tm": tm + 1}, device_id_type=mesh_ids)

    others_of(greet)

    def mask_rows(chunk, carry):
        rows = pl.ds(pl.multiple_of(chunk * CHUNK, CHUNK), CHUNK)
        across = lax.broadcasted_iota(jnp.int32, (CHUNK, chans), 1)
        down = lax.broadcasted_iota(jnp.int32, (CHUNK, chans), 0) + chunk * CHUNK
        live = jnp.broadcast_to(mask_ref[...].astype(jnp.float32), (CHUNK, chans))
        mask = jnp.sum(jnp.where(across == down, live, 0.0), axis=1, keepdims=True)
        mask = jnp.broadcast_to(mask, (CHUNK, LANES))

        def one(tile, carry):
            columns = pl.ds(pl.multiple_of(tile * LANES, LANES), LANES)
            held_signal[0, rows, columns] = (x_ref[rows, columns].astype(jnp.float32) * mask).astype(jnp.bfloat16)
            return carry

        return lax.fori_loop(0, span // LANES, one, carry, unroll=8)

    lax.fori_loop(0, chunks, mask_rows, 0)
    pl.semaphore_wait(barrier, ranks - 1 + jnp.where(tm > 0, 1, 0) + jnp.where(tm < blocks - 1, 1, 0))

    def halo_copy(to):
        return pltpu.make_async_remote_copy(
            src_ref=held_signal.at[0, :, pl.ds(0, SEG)],
            dst_ref=held_signal.at[0, :, pl.ds(span, SEG)],
            send_sem=halo_sems.at[0],
            recv_sem=halo_sems.at[1],
            device_id={"tm": to},
            device_id_type=mesh_ids,
        )

    def signal_copy(chunk):
        rows = pl.ds(pl.multiple_of(chunk * CHUNK, CHUNK), CHUNK)
        return pltpu.make_async_remote_copy(
            src_ref=held_signal.at[0, rows, pl.ds(0, span)],
            dst_ref=held_signal.at[1, rows, pl.ds(0, span)],
            send_sem=signal_sends.at[chunk],
            recv_sem=signal_recvs.at[chunk],
            device_id={"chan": mirror},
            device_id_type=mesh_ids,
        )

    def edge_copy(chunk, to):
        rows = pl.ds(pl.multiple_of(chunk * CHUNK, CHUNK), CHUNK)
        return pltpu.make_async_remote_copy(
            src_ref=held_signal.at[1, rows, pl.ds(0, SEG)],
            dst_ref=held_signal.at[1, rows, pl.ds(span, SEG)],
            send_sem=edge_sends.at[chunk],
            recv_sem=edge_recvs.at[chunk],
            device_id={"tm": to},
            device_id_type=mesh_ids,
        )

    def send_signal(chunk, carry):
        signal_copy(chunk).start()
        return carry

    @pl.when(tm > 0)
    def _():
        halo_copy(tm - 1).start()

    lax.fori_loop(0, 2, send_signal, 0)

    @pl.when(tm == blocks - 1)
    def _():
        held_signal[:, :, span:] = jnp.zeros((2, chans, SEG), jnp.bfloat16)

    for block in range(NP // LANES):
        row = slow_ref[:, block * LANES:(block + 1) * LANES].astype(jnp.float32)
        across = lax.broadcasted_iota(jnp.int32, (LANES, LANES), 1)
        down = lax.broadcasted_iota(jnp.int32, (LANES, LANES), 0)
        column = jnp.sum(jnp.where(across == down, jnp.broadcast_to(row, (LANES, LANES)), 0.0), axis=1, keepdims=True)
        slow[block * LANES:(block + 1) * LANES, :] = jnp.broadcast_to(column, (LANES, LANES)).astype(jnp.int32)

    @pl.when(tm < blocks - 1)
    def _():
        halo_copy(tm + 1).wait_recv()

    def block_copy(slot, chunk, origin, to):
        return pltpu.make_async_remote_copy(
            src_ref=send.at[slot, chunk, pl.ds(lax.rem(to, half) * own, own)],
            dst_ref=recv.at[chunk, origin],
            send_sem=send_sems.at[slot, chunk],
            recv_sem=recv_sems.at[chunk],
            device_id={"chan": to},
            device_id_type=mesh_ids,
        )

    def spectra(slot, chunk, origin):
        top = pl.multiple_of(chunk * CHUNK, CHUNK)

        def gather(s, carry):
            start = pl.multiple_of((s // 2) * LANES, LANES)
            back = LANES - (offs[s] - start)
            tiles = held_signal[slot, pl.ds(top, CHUNK), pl.ds(start, 3 * LANES)].astype(jnp.float32)
            a, b, c = [pltpu.roll(tiles[:, i * LANES:(i + 1) * LANES], back, 1) for i in range(3)]
            keep = lax.broadcasted_iota(jnp.int32, (CHUNK, LANES), 1) < back
            p0[pl.ds(s, CHUNK, stride=step), :] = jnp.where(keep, a, b)
            p1[pl.ds(s, CHUNK, stride=step), :] = jnp.where(keep, b, c)
            return carry

        lax.fori_loop(0, segs, gather, 0, unroll=128)
        table = table_ref[pl.ds(pl.multiple_of(side * NF, NF), NF), :]

        def transform(i, carry):
            pair = [pl.ds(pl.multiple_of((2 * i + part) * step, 8), segs) for part in range(2)]
            piece = jnp.concatenate([jnp.concatenate([p0[rows, :], p1[rows, :]], axis=1) for rows in pair]).astype(jnp.bfloat16)
            spec = lax.dot_general(table, piece, (((1,), (1,)), ((), ())), preferred_element_type=jnp.float32)
            for part in range(2):
                both = spec[:, part * segs:(part + 1) * segs]
                s0[pl.ds(2 * i + part, half_bins, stride=CHUNK + 8), :] = both[:half_bins]
                s1[pl.ds(2 * i + part, half_bins, stride=CHUNK + 8), :] = both[half_bins:]
            return carry

        lax.fori_loop(0, CHUNK // 2, transform, 0, unroll=8)

        def pack(f, carry):
            rows = pl.ds(pl.multiple_of(f * (CHUNK + 8), 8), CHUNK)
            send[slot, chunk, f] = jnp.concatenate([s0[rows, :], s1[rows, :]], axis=1).astype(jnp.bfloat16)
            return carry

        lax.fori_loop(0, half_bins, pack, 0, unroll=8)

        def launch(d, carry):
            block_copy(slot, chunk, origin, peer(ranks + half - d)).start()
            return carry

        lax.fori_loop(half + 1, ranks, launch, 0)
        recv[chunk, origin] = send[slot, chunk, pl.ds(lax.rem(me, half) * own, own)]

    def own_spectra(chunk, carry):
        spectra(0, chunk, me)
        return carry

    lax.fori_loop(0, chunks, own_spectra, 0)

    def steering(step, carry):
        f, rows = step // (NP // ROWS), lax.rem(step, NP // ROWS) * ROWS
        rows = pl.multiple_of(rows, ROWS)
        kp = (slow[pl.ds(rows, ROWS), :] * (me * own + f + 1)) & (modulus - 1)
        lane = lax.broadcasted_iota(jnp.int32, (ROWS, LANES), 1)
        first = (lane // CHUNK) * chans + (lane & (CHUNK - 1))
        scale = 1.0 / math.sqrt(total)
        cos0, sin0 = turn((kp * first) & (modulus - 1))
        cos0, sin0 = cos0 * scale, sin0 * scale
        hops = jnp.where(lane == 0, CHUNK, (LANES // CHUNK) * chans)
        cosp, sinp = turn((kp * hops) & (modulus - 1))
        rc, rs, bc, bs = [jnp.broadcast_to(v[:, i:i + 1], (ROWS, LANES)) for i in (0, 1) for v in (cosp, sinp)]
        for block in range(width // LANES):
            columns = slice(block * LANES, (block + 1) * LANES)
            cos, sin = cos0, sin0
            for chunk in range(chunks):
                steer[f, chunk, pl.ds(rows, ROWS), columns] = cos.astype(jnp.bfloat16)
                steer[f, chunk, pl.ds(NP + rows, ROWS), columns] = sin.astype(jnp.bfloat16)
                cos, sin = cos * rc - sin * rs, cos * rs + sin * rc
            cos0, sin0 = cos0 * bc - sin0 * bs, cos0 * bs + sin0 * bc
        return carry

    steps = own * (NP // ROWS)

    def mirror_spectra(chunk, carry):
        lax.fori_loop(steps * chunk // (2 * chunks), steps * (chunk + 1) // (2 * chunks), steering, 0)
        signal_copy(chunk).wait_send()

        @pl.when(chunk + 2 < chunks)
        def _():
            signal_copy(chunk + 2).start()

        signal_copy(chunk).wait_recv()

        @pl.when(tm > 0)
        def _():
            edge_copy(chunk, tm - 1).start()

        @pl.when(tm < blocks - 1)
        def _():
            edge_copy(chunk, tm + 1).wait_recv()

        spectra(1, chunk, mirror)
        return carry

    lax.fori_loop(0, chunks, mirror_spectra, 0)
    lax.fori_loop(steps // 2, steps, steering, 0)

    others = pl.ds(0, ranks - 1)

    def add(chunk, first, last):
        held = recv.at[chunk, pl.ds(0, ranks - 2)]
        pltpu.make_async_copy(held, held, recv_sems.at[chunk]).wait()

        def one_bin(f, carry):
            spec = recv[chunk, :, f].reshape(width, 2 * segs)
            both = jnp.dot(steer[f, chunk], spec, preferred_element_type=jnp.float32)
            real = both[:NP, :segs] - both[NP:, segs:]
            imag = both[:NP, segs:] + both[NP:, :segs]
            if not first:
                real, imag = beam_ref[f, 0] + real, beam_ref[f, 1] + imag
            beam_ref[f, 0] = real
            beam_ref[f, 1] = imag
            if last:
                energy[...] += real * real + imag * imag
            return carry

        lax.fori_loop(0, own, one_bin, 0, unroll=8)

    add(0, True, False)

    def more(chunk, carry):
        add(chunk, False, False)
        return carry

    lax.fori_loop(1, chunks - 1, more, 0)
    energy[...] = jnp.zeros((NP, segs), jnp.float32)
    add(chunks - 1, False, True)

    def power_copy(to):
        return pltpu.make_async_remote_copy(
            src_ref=terms.at[to],
            dst_ref=arrived.at[me],
            send_sem=power_sems.at[0],
            recv_sem=power_sems.at[1],
            device_id={"chan": to},
            device_id_type=pl.DeviceIdType.MESH,
        )

    def power_of(to):
        rows = pl.ds(pl.multiple_of(to * slows, slows), slows)

        return energy[rows, :] * (1.0 / NF)

    def power_term(d, carry):
        to = peer(d)
        terms[to] = power_of(to).astype(terms.dtype)
        power_copy(to).start()
        return carry

    others_of(power_term)
    arrived[me] = power_of(me).astype(arrived.dtype)
    pltpu.make_async_copy(arrived.at[others], arrived.at[others], power_sems.at[1]).wait()

    def sum_up(r, acc):
        return acc + arrived[r].astype(jnp.float32)

    power_ref[...] = lax.fori_loop(0, ranks, sum_up, jnp.zeros((slows, segs), jnp.float32))

    def finish(chunk, carry):
        sent = recv.at[chunk, pl.ds(0, half - 1)]
        pltpu.make_async_copy(sent, sent, send_sems.at[0, chunk]).wait()
        pltpu.make_async_copy(sent, sent, send_sems.at[1, chunk]).wait()

        @pl.when(tm > 0)
        def _():
            edge_copy(chunk, tm - 1).wait_send()

        return carry

    lax.fori_loop(0, chunks, finish, 0)
    pltpu.make_async_copy(terms.at[others], terms.at[others], power_sems.at[0]).wait()

    @pl.when(tm > 0)
    def _():
        halo_copy(tm - 1).wait_send()


def fused(signal, mask, offsets, table, slow, ranks, blocks):
    chans, segs = signal.shape[0], offsets.shape[0]
    slows = NP // ranks
    term = jnp.bfloat16 if slows % 16 == 0 else jnp.float32
    own, chunks = NF // ranks, chans // CHUNK
    vmem = pl.BlockSpec(memory_space=pltpu.VMEM)
    return pl.pallas_call(
        functools.partial(fused_kernel, ranks=ranks, blocks=blocks),
        out_shape=(
            pltpu.VMEM((own, 2, NP, segs), jnp.float32),
            pltpu.VMEM((NP // ranks, segs), jnp.float32),
        ),
        in_specs=[pl.BlockSpec(memory_space=pltpu.SMEM), vmem, vmem, vmem, vmem],
        out_specs=(vmem, vmem),
        scratch_shapes=[
            pltpu.VMEM((NP, LANES), jnp.int32),
            pltpu.VMEM((2, chans, signal.shape[1] + SEG), jnp.bfloat16),
        ]
        + [pltpu.VMEM((CHUNK * (segs + PAD), LANES), jnp.float32)] * 2
        + [pltpu.VMEM((NF // 2 * (CHUNK + 8), segs), jnp.float32)] * 2
        + [
            pltpu.VMEM((2, chunks, NF // 2, CHUNK, 2 * segs), jnp.bfloat16),
            pltpu.VMEM((chunks, ranks, own, CHUNK, 2 * segs), jnp.bfloat16),
            pltpu.VMEM((own, chunks, 2 * NP, ranks * CHUNK), jnp.bfloat16),
            pltpu.VMEM((NP, segs), jnp.float32),
            pltpu.VMEM((ranks, slows, segs), term),
            pltpu.VMEM((ranks, slows, segs), term),
            pltpu.SemaphoreType.DMA((2, chunks)),
            pltpu.SemaphoreType.DMA((chunks,)),
            pltpu.SemaphoreType.DMA((2,)),
            pltpu.SemaphoreType.DMA((2,)),
            pltpu.SemaphoreType.DMA((chunks,)),
            pltpu.SemaphoreType.DMA((chunks,)),
            pltpu.SemaphoreType.DMA((chunks,)),
            pltpu.SemaphoreType.DMA((chunks,)),
        ],
        compiler_params=pltpu.CompilerParams(vmem_limit_bytes=VMEM_LIMIT, collective_id=0, has_side_effects=True),
        cost_estimate=pl.CostEstimate(flops=7 << 30, bytes_accessed=8 << 20, transcendentals=0),
        name="beamform",
    )(*[pltpu.with_memory_space_constraint(x, pltpu.HBM) for x in (offsets, signal, mask, table, slow)])


def store_kernel(beam_ref, power_ref, beam_out, power_out, sems):
    bins = beam_ref.shape[0]

    def copy(f):
        return pltpu.make_async_copy(beam_ref.at[f], beam_out.at[f], sems.at[f])

    last = pltpu.make_async_copy(power_ref, power_out, sems.at[bins])
    for f in range(bins):
        copy(f).start()
    last.start()
    for f in range(bins):
        copy(f).wait()
    last.wait()


def store(beam, power):
    vmem, anywhere = pl.BlockSpec(memory_space=pltpu.VMEM), pl.BlockSpec(memory_space=pl.ANY)
    return pl.pallas_call(
        store_kernel,
        out_shape=(jax.ShapeDtypeStruct(beam.shape, beam.dtype), jax.ShapeDtypeStruct(power.shape, power.dtype)),
        in_specs=[vmem, vmem],
        out_specs=(anywhere, anywhere),
        scratch_shapes=[pltpu.SemaphoreType.DMA((beam.shape[0] + 1,))],
        cost_estimate=pl.CostEstimate(flops=0, bytes_accessed=2 * beam.size * 4, transcendentals=0),
        compiler_params=pltpu.CompilerParams(vmem_limit_bytes=8 << 20),
        name="store",
    )(*[pltpu.with_memory_space_constraint(x, pltpu.VMEM) for x in (beam, power)])


def local(signal, channel_mask, seg_offsets, slow_steps):
    ranks, blocks = lax.axis_size("chan"), lax.axis_size("tm")
    return store(*fused(signal, channel_mask[None, :], seg_offsets, make_table(), slow_steps[None, :], ranks, blocks))


def solution(mesh):
    in_specs = (P("chan", "tm"), P("chan"), P("tm"), P())
    out_specs = (P("chan", None, None, "tm"), P("chan", "tm"))
    return jax.shard_map(local, mesh=mesh, in_specs=in_specs, out_specs=out_specs, check_vma=False)
```

```python
import functools
import math

import jax
import jax.numpy as jnp
import ml_dtypes
import numpy as np
from jax import lax
from jax.experimental import pallas as pl
from jax.experimental.pallas import tpu as pltpu
from jax.sharding import PartitionSpec as P

SEG = 256
NF = 128
NP = 512
SUBSTEPS = 16
HOP = 64
LANES = 128
CHUNK = 16
ROWS = 64
PAD = 8
VMEM_LIMIT = 46 * 1024 * 1024


def make_table():
    points = np.arange(SEG)
    bins = np.arange(1, NF + 1)
    taper = 0.5 - 0.5 * np.cos(2.0 * np.pi * points / SEG)
    angle = ((bins[:, None] * points[None, :]) % SEG) * (2.0 * np.pi / SEG)
    scale = 1.0 / math.sqrt(3.0 * SEG / 8.0)
    table = np.stack([taper * np.cos(angle), -taper * np.sin(angle)]).reshape(2, 2, NF // 2, SEG) * scale
    table = table.transpose(1, 0, 2, 3).reshape(2 * NF, SEG)
    return jnp.asarray(table.astype(np.float32).astype(ml_dtypes.bfloat16))


def turn(index):
    quarter = SEG * SUBSTEPS // 4
    quadrant = (index + quarter // 2) >> 10
    x = (index - quadrant * quarter).astype(jnp.float32) * (0.5 * math.pi / quarter)
    y = x * x
    sin = x * (1.0 + y * (-1.0 / 6 + y * (1.0 / 120 + y * (-1.0 / 5040 + y * (1.0 / 362880)))))
    cos = 1.0 + y * (-0.5 + y * (1.0 / 24 + y * (-1.0 / 720 + y * (1.0 / 40320))))
    odd = (quadrant & 1) == 1
    c, d = jnp.where(odd, sin, cos), jnp.where(odd, cos, sin)
    return jnp.where(((quadrant + 1) & 2) == 2, -c, c), jnp.where((quadrant & 2) == 2, -d, d)


def fused_kernel(offsets_ref, signal_ref, channel_mask_ref, taper_ref, steps_ref, beam_ref, power_ref, offs, mask_ref, table_ref, slow_ref, x_ref, slow, held_signal, p0, p1, s0, s1, send, recv, steer, energy, terms, arrived, send_sems, recv_sems, power_sems, halo_sems, signal_sends, signal_recvs, edge_sends, edge_recvs, load_sems, small_sems, *, ranks, blocks):
    chans = signal_ref.shape[0]
    chunks = chans // CHUNK
    step = p0.shape[0] // CHUNK
    segs = step - PAD
    own = NF // ranks
    slows = NP // ranks
    width = ranks * CHUNK
    total = chans * ranks
    modulus = SEG * SUBSTEPS
    me = lax.axis_index("chan")

    tm = lax.axis_index("tm")
    half = ranks // 2
    side = me // half
    mirror = (1 - side) * half + lax.rem(me, half)
    span = signal_ref.shape[1]
    half_bins = NF // 2

    def peer(d):
        return (1 - side + d // half) % 2 * half + ((me % half) ^ (d % half))

    barrier = pltpu.get_barrier_semaphore()
    mesh_ids = pl.DeviceIdType.MESH

    smalls = ((channel_mask_ref, mask_ref), (taper_ref, table_ref), (offsets_ref, offs), (steps_ref, slow_ref))
    load_mask, load_table, load_offsets, load_steps = [pltpu.make_async_copy(*pair, small_sems.at[i]) for i, pair in enumerate(smalls)]
    load_mask.start()
    for chunk in range(chunks):
        rows = pl.ds(chunk * CHUNK, CHUNK)
        pltpu.make_async_copy(signal_ref.at[rows], x_ref.at[rows], load_sems.at[chunk]).start()

    load_table.start()
    load_offsets.start()
    load_steps.start()

    def greet(d, carry):
        pl.semaphore_signal(barrier, inc=1, device_id={"chan": peer(d)}, device_id_type=mesh_ids)
        return carry

    def others_of(body):
        lax.fori_loop(0, half, body, 0, unroll=8)
        lax.fori_loop(half + 1, ranks, body, 0, unroll=min(7, half - 1))

    @pl.when(tm > 0)
    def _():
        pl.semaphore_signal(barrier, inc=1, device_id={"tm": tm - 1}, device_id_type=mesh_ids)

    @pl.when(tm < blocks - 1)
    def _():
        pl.semaphore_signal(barrier, inc=1, device_id={"tm": tm + 1}, device_id_type=mesh_ids)

    others_of(greet)

    def load(chunk):
        rows = pl.ds(pl.multiple_of(chunk * CHUNK, CHUNK), CHUNK)
        return pltpu.make_async_copy(signal_ref.at[rows], x_ref.at[rows], load_sems.at[chunk])

    def mask_rows(chunk, carry):
        load(chunk).wait()
        rows = pl.ds(pl.multiple_of(chunk * CHUNK, CHUNK), CHUNK)
        across = lax.broadcasted_iota(jnp.int32, (CHUNK, chans), 1)
        down = lax.broadcasted_iota(jnp.int32, (CHUNK, chans), 0) + chunk * CHUNK
        live = jnp.broadcast_to(mask_ref[...].astype(jnp.float32), (CHUNK, chans))
        mask = jnp.sum(jnp.where(across == down, live, 0.0), axis=1, keepdims=True)
        mask = jnp.broadcast_to(mask, (CHUNK, LANES)).astype(jnp.bfloat16)

        def one(tile, carry):
            columns = pl.ds(pl.multiple_of(tile * LANES, LANES), LANES)
            held_signal[0, rows, columns] = x_ref[rows, columns] * mask
            return carry

        return lax.fori_loop(0, span // LANES, one, carry, unroll=8)

    load_mask.wait()
    lax.fori_loop(0, 2, mask_rows, 0)
    pl.semaphore_wait(barrier, ranks - 1 + jnp.where(tm > 0, 1, 0) + jnp.where(tm < blocks - 1, 1, 0))

    def halo_copy(to):
        return pltpu.make_async_remote_copy(
            src_ref=held_signal.at[0, :, pl.ds(0, SEG)],
            dst_ref=held_signal.at[0, :, pl.ds(span, SEG)],
            send_sem=halo_sems.at[0],
            recv_sem=halo_sems.at[1],
            device_id={"tm": to},
            device_id_type=mesh_ids,
        )

    def signal_copy(chunk):
        rows = pl.ds(pl.multiple_of(chunk * CHUNK, CHUNK), CHUNK)
        return pltpu.make_async_remote_copy(
            src_ref=held_signal.at[0, rows, pl.ds(0, span)],
            dst_ref=held_signal.at[1, rows, pl.ds(0, span)],
            send_sem=signal_sends.at[chunk],
            recv_sem=signal_recvs.at[chunk],
            device_id={"chan": mirror},
            device_id_type=mesh_ids,
        )

    def edge_copy(chunk, to):
        rows = pl.ds(pl.multiple_of(chunk * CHUNK, CHUNK), CHUNK)
        return pltpu.make_async_remote_copy(
            src_ref=held_signal.at[1, rows, pl.ds(0, SEG)],
            dst_ref=held_signal.at[1, rows, pl.ds(span, SEG)],
            send_sem=edge_sends.at[chunk],
            recv_sem=edge_recvs.at[chunk],
            device_id={"tm": to},
            device_id_type=mesh_ids,
        )

    def send_signal(chunk, carry):
        signal_copy(chunk).start()
        return carry

    lax.fori_loop(0, 2, send_signal, 0)
    lax.fori_loop(2, chunks, mask_rows, 0)

    @pl.when(tm > 0)
    def _():
        halo_copy(tm - 1).start()


    @pl.when(tm == blocks - 1)
    def _():
        held_signal[:, :, span:] = jnp.zeros((2, chans, SEG), jnp.bfloat16)

    @pl.when(tm < blocks - 1)
    def _():
        halo_copy(tm + 1).wait_recv()

    def block_copy(slot, chunk, origin, to):
        return pltpu.make_async_remote_copy(
            src_ref=send.at[slot, chunk, pl.ds(lax.rem(to, half) * own, own)],
            dst_ref=recv.at[chunk, origin],
            send_sem=send_sems.at[slot, chunk],
            recv_sem=recv_sems.at[chunk],
            device_id={"chan": to},
            device_id_type=mesh_ids,
        )

    def spectra(slot, chunk, origin):
        top = pl.multiple_of(chunk * CHUNK, CHUNK)

        def gather(s, carry):
            start = pl.multiple_of((s // 2) * LANES, LANES)
            back = LANES - (offs[s] - start)
            tiles = held_signal[slot, pl.ds(top, CHUNK), pl.ds(start, 3 * LANES)].astype(jnp.float32)
            a, b, c = [pltpu.roll(tiles[:, i * LANES:(i + 1) * LANES], back, 1) for i in range(3)]
            keep = lax.broadcasted_iota(jnp.int32, (CHUNK, LANES), 1) < back
            p0[pl.ds(s, CHUNK, stride=step), :] = jnp.where(keep, a, b)
            p1[pl.ds(s, CHUNK, stride=step), :] = jnp.where(keep, b, c)
            return carry

        lax.fori_loop(0, segs, gather, 0, unroll=128)
        table = table_ref[pl.ds(pl.multiple_of(side * NF, NF), NF), :]

        def transform(i, carry):
            pair = [pl.ds(pl.multiple_of((2 * i + part) * step, 8), segs) for part in range(2)]
            piece = jnp.concatenate([jnp.concatenate([p0[rows, :], p1[rows, :]], axis=1) for rows in pair]).astype(jnp.bfloat16)
            spec = lax.dot_general(table, piece, (((1,), (1,)), ((), ())), preferred_element_type=jnp.float32)
            for part in range(2):
                both = spec[:, part * segs:(part + 1) * segs]
                s0[pl.ds(2 * i + part, half_bins, stride=CHUNK + 8), :] = both[:half_bins]
                s1[pl.ds(2 * i + part, half_bins, stride=CHUNK + 8), :] = both[half_bins:]
            return carry

        lax.fori_loop(0, CHUNK // 2, transform, 0, unroll=8)

        def pack(f, carry):
            rows = pl.ds(pl.multiple_of(f * (CHUNK + 8), 8), CHUNK)
            send[slot, chunk, f] = jnp.concatenate([s0[rows, :], s1[rows, :]], axis=1).astype(jnp.bfloat16)
            return carry

        lax.fori_loop(0, half_bins, pack, 0, unroll=8)

        def launch(d, carry):
            block_copy(slot, chunk, origin, peer(ranks + half - d)).start()
            return carry

        lax.fori_loop(half + 1, ranks, launch, 0)
        recv[chunk, origin] = send[slot, chunk, pl.ds(lax.rem(me, half) * own, own)]

    load_table.wait()
    load_offsets.wait()
    load_steps.wait()

    def own_spectra(chunk, carry):
        spectra(0, chunk, me)
        return carry

    lax.fori_loop(0, chunks, own_spectra, 0)

    for block in range(NP // LANES):
        row = slow_ref[:, block * LANES:(block + 1) * LANES].astype(jnp.float32)
        across = lax.broadcasted_iota(jnp.int32, (LANES, LANES), 1)
        down = lax.broadcasted_iota(jnp.int32, (LANES, LANES), 0)
        column = jnp.sum(jnp.where(across == down, jnp.broadcast_to(row, (LANES, LANES)), 0.0), axis=1, keepdims=True)
        slow[block * LANES:(block + 1) * LANES, :] = jnp.broadcast_to(column, (LANES, LANES)).astype(jnp.int32)

    def steering(step, carry):
        f, rows = step // (NP // ROWS), lax.rem(step, NP // ROWS) * ROWS
        rows = pl.multiple_of(rows, ROWS)
        kp = (slow[pl.ds(rows, ROWS), :] * (me * own + f + 1)) & (modulus - 1)
        lane = lax.broadcasted_iota(jnp.int32, (ROWS, LANES), 1)
        first = (lane // CHUNK) * chans + (lane & (CHUNK - 1))
        scale = 1.0 / math.sqrt(total)
        cos0, sin0 = turn((kp * first) & (modulus - 1))
        cos0, sin0 = cos0 * scale, sin0 * scale
        hops = jnp.where(lane == 0, CHUNK, (LANES // CHUNK) * chans)
        cosp, sinp = turn((kp * hops) & (modulus - 1))
        rc, rs, bc, bs = [jnp.broadcast_to(v[:, i:i + 1], (ROWS, LANES)) for i in (0, 1) for v in (cosp, sinp)]
        for block in range(width // LANES):
            columns = slice(block * LANES, (block + 1) * LANES)
            cos, sin = cos0, sin0
            for chunk in range(chunks):
                steer[f, chunk, pl.ds(rows, ROWS), columns] = cos.astype(jnp.bfloat16)
                steer[f, chunk, pl.ds(NP + rows, ROWS), columns] = sin.astype(jnp.bfloat16)
                cos, sin = cos * rc - sin * rs, cos * rs + sin * rc
            cos0, sin0 = cos0 * bc - sin0 * bs, cos0 * bs + sin0 * bc
        return carry

    steps = own * (NP // ROWS)

    def mirror_spectra(chunk, carry):
        lax.fori_loop(steps * chunk // (2 * chunks), steps * (chunk + 1) // (2 * chunks), steering, 0)
        signal_copy(chunk).wait_send()

        @pl.when(chunk + 2 < chunks)
        def _():
            signal_copy(chunk + 2).start()

        signal_copy(chunk).wait_recv()

        @pl.when(tm > 0)
        def _():
            edge_copy(chunk, tm - 1).start()

        @pl.when(tm < blocks - 1)
        def _():
            edge_copy(chunk, tm + 1).wait_recv()

        spectra(1, chunk, mirror)
        return carry

    lax.fori_loop(0, chunks, mirror_spectra, 0)
    lax.fori_loop(steps // 2, steps, steering, 0)

    others = pl.ds(0, ranks - 1)

    def arrivals(chunk):
        held = recv.at[chunk, pl.ds(0, ranks - 2)]
        pltpu.make_async_copy(held, held, recv_sems.at[chunk]).wait()

    def add(chunk, first):
        arrivals(chunk)

        def one_bin(f, carry):
            spec = recv[chunk, :, f].reshape(width, 2 * segs)
            both = jnp.dot(steer[f, chunk], spec, preferred_element_type=jnp.float32)
            real = both[:NP, :segs] - both[NP:, segs:]
            imag = both[:NP, segs:] + both[NP:, :segs]
            beam_ref[f, 0] = real if first else beam_ref[f, 0] + real
            beam_ref[f, 1] = imag if first else beam_ref[f, 1] + imag
            return carry

        lax.fori_loop(0, own, one_bin, 0, unroll=8)

    add(0, True)

    def more(chunk, carry):
        add(chunk, False)
        return carry

    lax.fori_loop(1, chunks - 1, more, 0)

    def power_copy(to):
        return pltpu.make_async_remote_copy(
            src_ref=terms.at[to],
            dst_ref=arrived.at[me],
            send_sem=power_sems.at[0],
            recv_sem=power_sems.at[1],
            device_id={"chan": to},
            device_id_type=pl.DeviceIdType.MESH,
        )

    last = chunks - 1
    rows_of_side = NP // 2
    energy[...] = jnp.zeros((rows_of_side, segs), jnp.float32)
    arrivals(last)

    def finish_side(phase, carry):
        owners = lax.rem(side + 1 + phase, 2)
        base = pl.multiple_of(owners * rows_of_side, rows_of_side)
        rows = pl.ds(base, rows_of_side)

        def one_bin(f, acc):
            spec = recv[last, :, f].reshape(width, 2 * segs)
            both = jnp.concatenate([steer[f, last, pl.ds(base + part * NP, rows_of_side), :] for part in range(2)])
            both = jnp.dot(both, spec, preferred_element_type=jnp.float32)
            real = beam_ref[f, 0, rows, :] + (both[:rows_of_side, :segs] - both[rows_of_side:, segs:])
            imag = beam_ref[f, 1, rows, :] + (both[:rows_of_side, segs:] + both[rows_of_side:, :segs])
            beam_ref[f, 0, rows, :] = real
            beam_ref[f, 1, rows, :] = imag
            energy[...] = jnp.where(f == 0, 0.0, energy[...]) + (real * real + imag * imag)
            return acc

        lax.fori_loop(0, own, one_bin, 0, unroll=8)
        mine = terms.at[pl.ds(owners * half, half)]
        mine[...] = (energy[...] * (1.0 / NF)).reshape(half, slows, segs).astype(terms.dtype)

        def power_term(d, carry):
            power_copy(peer(half - 1 - d + phase * (ranks + 1))).start()
            return carry

        lax.fori_loop(phase * (half + 1), half + phase * half, power_term, 0)
        return carry

    lax.fori_loop(0, 2, finish_side, 0)
    arrived[me] = terms[me]
    pltpu.make_async_copy(arrived.at[others], arrived.at[others], power_sems.at[1]).wait()

    def sum_up(r, acc):
        return acc + arrived[r].astype(jnp.float32)

    power_ref[...] = lax.fori_loop(0, ranks, sum_up, jnp.zeros((slows, segs), jnp.float32))

    def finish(chunk, carry):
        sent = recv.at[chunk, pl.ds(0, half - 1)]
        pltpu.make_async_copy(sent, sent, send_sems.at[0, chunk]).wait()
        pltpu.make_async_copy(sent, sent, send_sems.at[1, chunk]).wait()

        @pl.when(tm > 0)
        def _():
            edge_copy(chunk, tm - 1).wait_send()

        return carry

    lax.fori_loop(0, chunks, finish, 0)
    pltpu.make_async_copy(terms.at[others], terms.at[others], power_sems.at[0]).wait()

    @pl.when(tm > 0)
    def _():
        halo_copy(tm - 1).wait_send()


def fused(signal, mask, offsets, table, slow, ranks, blocks):
    chans, segs = signal.shape[0], offsets.shape[0]
    slows = NP // ranks
    term = jnp.bfloat16 if slows % 16 == 0 else jnp.float32
    own, chunks = NF // ranks, chans // CHUNK
    vmem = pl.BlockSpec(memory_space=pltpu.VMEM)
    return pl.pallas_call(
        functools.partial(fused_kernel, ranks=ranks, blocks=blocks),
        out_shape=(
            pltpu.VMEM((own, 2, NP, segs), jnp.float32),
            pltpu.VMEM((NP // ranks, segs), jnp.float32),
        ),
        in_specs=[pl.BlockSpec(memory_space=pl.ANY)] * 5,
        out_specs=(vmem, vmem),
        scratch_shapes=[
            pltpu.SMEM(offsets.shape, offsets.dtype),
            pltpu.VMEM(mask.shape, mask.dtype),
            pltpu.VMEM(table.shape, table.dtype),
            pltpu.VMEM(slow.shape, slow.dtype),
            pltpu.VMEM(signal.shape, signal.dtype),
            pltpu.VMEM((NP, LANES), jnp.int32),
            pltpu.VMEM((2, chans, signal.shape[1] + SEG), jnp.bfloat16),
        ]
        + [pltpu.VMEM((CHUNK * (segs + PAD), LANES), jnp.float32)] * 2
        + [pltpu.VMEM((NF // 2 * (CHUNK + 8), segs), jnp.float32)] * 2
        + [
            pltpu.VMEM((2, chunks, NF // 2, CHUNK, 2 * segs), jnp.bfloat16),
            pltpu.VMEM((chunks, ranks, own, CHUNK, 2 * segs), jnp.bfloat16),
            pltpu.VMEM((own, chunks, 2 * NP, ranks * CHUNK), jnp.bfloat16),
            pltpu.VMEM((NP // 2, segs), jnp.float32),
            pltpu.VMEM((ranks, slows, segs), term),
            pltpu.VMEM((ranks, slows, segs), term),
            pltpu.SemaphoreType.DMA((2, chunks)),
            pltpu.SemaphoreType.DMA((chunks,)),
            pltpu.SemaphoreType.DMA((2,)),
            pltpu.SemaphoreType.DMA((2,)),
            pltpu.SemaphoreType.DMA((chunks,)),
            pltpu.SemaphoreType.DMA((chunks,)),
            pltpu.SemaphoreType.DMA((chunks,)),
            pltpu.SemaphoreType.DMA((chunks,)),
            pltpu.SemaphoreType.DMA((chunks,)),
            pltpu.SemaphoreType.DMA((4,)),
        ],
        compiler_params=pltpu.CompilerParams(vmem_limit_bytes=VMEM_LIMIT, collective_id=0, has_side_effects=True),
        cost_estimate=pl.CostEstimate(flops=7 << 30, bytes_accessed=8 << 20, transcendentals=0),
        name="beamform",
    )(*[pltpu.with_memory_space_constraint(x, pltpu.HBM) for x in (offsets, signal, mask, table, slow)])


def store_kernel(beam_ref, power_ref, beam_out, power_out, sems):
    bins = beam_ref.shape[0]

    def copy(f):
        return pltpu.make_async_copy(beam_ref.at[f], beam_out.at[f], sems.at[f])

    last = pltpu.make_async_copy(power_ref, power_out, sems.at[bins])
    for f in range(bins):
        copy(f).start()
    last.start()
    for f in range(bins):
        copy(f).wait()
    last.wait()


def store(beam, power):
    vmem, anywhere = pl.BlockSpec(memory_space=pltpu.VMEM), pl.BlockSpec(memory_space=pl.ANY)
    return pl.pallas_call(
        store_kernel,
        out_shape=(jax.ShapeDtypeStruct(beam.shape, beam.dtype), jax.ShapeDtypeStruct(power.shape, power.dtype)),
        in_specs=[vmem, vmem],
        out_specs=(anywhere, anywhere),
        scratch_shapes=[pltpu.SemaphoreType.DMA((beam.shape[0] + 1,))],
        cost_estimate=pl.CostEstimate(flops=0, bytes_accessed=2 * beam.size * 4, transcendentals=0),
        compiler_params=pltpu.CompilerParams(vmem_limit_bytes=8 << 20),
        name="store",
    )(*[pltpu.with_memory_space_constraint(x, pltpu.VMEM) for x in (beam, power)])


def local(signal, channel_mask, seg_offsets, slow_steps):
    ranks, blocks = lax.axis_size("chan"), lax.axis_size("tm")
    return store(*fused(signal, channel_mask[None, :], seg_offsets, make_table(), slow_steps[None, :], ranks, blocks))


def solution(mesh):
    in_specs = (P("chan", "tm"), P("chan"), P("tm"), P())
    out_specs = (P("chan", None, None, "tm"), P("chan", "tm"))
    return jax.shard_map(local, mesh=mesh, in_specs=in_specs, out_specs=out_specs, check_vma=False)
```

```python
import functools
import math

import jax
import jax.numpy as jnp
import ml_dtypes
import numpy as np
from jax import lax
from jax.experimental import pallas as pl
from jax.experimental.pallas import tpu as pltpu
from jax.sharding import PartitionSpec as P

SEG = 256
NF = 128
NP = 512
SUBSTEPS = 16
HOP = 64
LANES = 128
CHUNK = 16
ROWS = 64
PAD = 8
VMEM_LIMIT = 46 * 1024 * 1024


def make_table():
    points = np.arange(SEG)
    bins = np.arange(1, NF + 1)
    taper = 0.5 - 0.5 * np.cos(2.0 * np.pi * points / SEG)
    angle = ((bins[:, None] * points[None, :]) % SEG) * (2.0 * np.pi / SEG)
    scale = 1.0 / math.sqrt(3.0 * SEG / 8.0)
    table = np.stack([taper * np.cos(angle), -taper * np.sin(angle)]).reshape(2, 2, NF // 2, SEG) * scale
    table = table.transpose(1, 0, 2, 3).reshape(2 * NF, SEG)
    return jnp.asarray(table.astype(np.float32).astype(ml_dtypes.bfloat16))


def turn(index):
    quarter = SEG * SUBSTEPS // 4
    quadrant = (index + quarter // 2) >> 10
    x = (index - quadrant * quarter).astype(jnp.float32) * (0.5 * math.pi / quarter)
    y = x * x
    sin = x * (1.0 + y * (-1.0 / 6 + y * (1.0 / 120 + y * (-1.0 / 5040 + y * (1.0 / 362880)))))
    cos = 1.0 + y * (-0.5 + y * (1.0 / 24 + y * (-1.0 / 720 + y * (1.0 / 40320))))
    odd = (quadrant & 1) == 1
    c, d = jnp.where(odd, sin, cos), jnp.where(odd, cos, sin)
    return jnp.where(((quadrant + 1) & 2) == 2, -c, c), jnp.where((quadrant & 2) == 2, -d, d)


def fused_kernel(offsets_ref, signal_ref, channel_mask_ref, taper_ref, steps_ref, beam_ref, power_ref, offs, mask_ref, table_ref, slow_ref, x_ref, slow, held_signal, p0, p1, s0, s1, send, recv, steer, energy, terms, arrived, send_sems, recv_sems, power_sems, halo_sems, signal_sends, signal_recvs, edge_sends, edge_recvs, load_sems, small_sems, *, ranks, blocks):
    chans = signal_ref.shape[0]
    chunks = chans // CHUNK
    step = p0.shape[0] // CHUNK
    segs = step - PAD
    own = NF // ranks
    slows = NP // ranks
    width = ranks * CHUNK
    total = chans * ranks
    modulus = SEG * SUBSTEPS
    me = lax.axis_index("chan")

    tm = lax.axis_index("tm")
    half = ranks // 2
    side = me // half
    mirror = (1 - side) * half + lax.rem(me, half)
    span = signal_ref.shape[1]
    half_bins = NF // 2

    def peer(d):
        return (1 - side + d // half) % 2 * half + ((me % half) ^ (d % half))

    barrier = pltpu.get_barrier_semaphore()
    mesh_ids = pl.DeviceIdType.MESH

    smalls = ((channel_mask_ref, mask_ref), (taper_ref, table_ref), (offsets_ref, offs), (steps_ref, slow_ref))
    load_mask, load_table, load_offsets, load_steps = [pltpu.make_async_copy(*pair, small_sems.at[i]) for i, pair in enumerate(smalls)]
    load_mask.start()
    for chunk in range(chunks):
        rows = pl.ds(chunk * CHUNK, CHUNK)
        pltpu.make_async_copy(signal_ref.at[rows], x_ref.at[rows], load_sems.at[chunk]).start()

    load_table.start()
    load_offsets.start()
    load_steps.start()

    def greet(d, carry):
        pl.semaphore_signal(barrier, inc=1, device_id={"chan": peer(d)}, device_id_type=mesh_ids)
        return carry

    def others_of(body):
        lax.fori_loop(0, half, body, 0, unroll=8)
        lax.fori_loop(half + 1, ranks, body, 0, unroll=min(7, half - 1))

    @pl.when(tm > 0)
    def _():
        pl.semaphore_signal(barrier, inc=1, device_id={"tm": tm - 1}, device_id_type=mesh_ids)

    @pl.when(tm < blocks - 1)
    def _():
        pl.semaphore_signal(barrier, inc=1, device_id={"tm": tm + 1}, device_id_type=mesh_ids)

    others_of(greet)

    def load(chunk):
        rows = pl.ds(pl.multiple_of(chunk * CHUNK, CHUNK), CHUNK)
        return pltpu.make_async_copy(signal_ref.at[rows], x_ref.at[rows], load_sems.at[chunk])

    edge = SEG // LANES

    def mask_tiles(chunk, low, high):
        rows = pl.ds(pl.multiple_of(chunk * CHUNK, CHUNK), CHUNK)
        across = lax.broadcasted_iota(jnp.int32, (CHUNK, chans), 1)
        down = lax.broadcasted_iota(jnp.int32, (CHUNK, chans), 0) + chunk * CHUNK
        live = jnp.broadcast_to(mask_ref[...].astype(jnp.float32), (CHUNK, chans))
        mask = jnp.sum(jnp.where(across == down, live, 0.0), axis=1, keepdims=True)
        mask = jnp.broadcast_to(mask, (CHUNK, LANES)).astype(jnp.bfloat16)

        def one(tile, carry):
            columns = pl.ds(pl.multiple_of(tile * LANES, LANES), LANES)
            held_signal[0, rows, columns] = x_ref[rows, columns] * mask
            return carry

        lax.fori_loop(low, high, one, 0, unroll=(high - low) // 2)

    def mask_edge(chunk, carry):
        load(chunk).wait()
        mask_tiles(chunk, 0, edge)
        return carry

    def mask_rows(chunk, carry):
        mask_tiles(chunk, edge, span // LANES)
        return carry

    load_mask.wait()
    lax.fori_loop(0, chunks, mask_edge, 0)
    lax.fori_loop(0, 2, mask_rows, 0)
    pl.semaphore_wait(barrier, ranks - 1 + jnp.where(tm > 0, 1, 0) + jnp.where(tm < blocks - 1, 1, 0))

    def halo_copy(to):
        return pltpu.make_async_remote_copy(
            src_ref=held_signal.at[0, :, pl.ds(0, SEG)],
            dst_ref=held_signal.at[0, :, pl.ds(span, SEG)],
            send_sem=halo_sems.at[0],
            recv_sem=halo_sems.at[1],
            device_id={"tm": to},
            device_id_type=mesh_ids,
        )

    def signal_copy(chunk):
        rows = pl.ds(pl.multiple_of(chunk * CHUNK, CHUNK), CHUNK)
        return pltpu.make_async_remote_copy(
            src_ref=held_signal.at[0, rows, pl.ds(0, span)],
            dst_ref=held_signal.at[1, rows, pl.ds(0, span)],
            send_sem=signal_sends.at[chunk],
            recv_sem=signal_recvs.at[chunk],
            device_id={"chan": mirror},
            device_id_type=mesh_ids,
        )

    def edge_copy(chunk, to):
        rows = pl.ds(pl.multiple_of(chunk * CHUNK, CHUNK), CHUNK)
        return pltpu.make_async_remote_copy(
            src_ref=held_signal.at[1, rows, pl.ds(0, SEG)],
            dst_ref=held_signal.at[1, rows, pl.ds(span, SEG)],
            send_sem=edge_sends.at[chunk],
            recv_sem=edge_recvs.at[chunk],
            device_id={"tm": to},
            device_id_type=mesh_ids,
        )

    def send_signal(chunk, carry):
        signal_copy(chunk).start()
        return carry

    @pl.when(tm > 0)
    def _():
        halo_copy(tm - 1).start()

    lax.fori_loop(0, 2, send_signal, 0)
    lax.fori_loop(2, chunks, mask_rows, 0)

    @pl.when(tm == blocks - 1)
    def _():
        held_signal[:, :, span:] = jnp.zeros((2, chans, SEG), jnp.bfloat16)

    def block_copy(slot, chunk, origin, to):
        return pltpu.make_async_remote_copy(
            src_ref=send.at[slot, chunk, pl.ds(lax.rem(to, half) * own, own)],
            dst_ref=recv.at[chunk, origin],
            send_sem=send_sems.at[slot, chunk],
            recv_sem=recv_sems.at[slot, chunk],
            device_id={"chan": to},
            device_id_type=mesh_ids,
        )

    inner = 2 * ((span - 3 * LANES) // LANES + 1)

    def spectra(slot, chunk, origin, edge_ready):
        top = pl.multiple_of(chunk * CHUNK, CHUNK)

        def gather(s, carry):
            start = pl.multiple_of((s // 2) * LANES, LANES)
            back = LANES - (offs[s] - start)
            tiles = held_signal[slot, pl.ds(top, CHUNK), pl.ds(start, 3 * LANES)].astype(jnp.float32)
            a, b, c = [pltpu.roll(tiles[:, i * LANES:(i + 1) * LANES], back, 1) for i in range(3)]
            keep = lax.broadcasted_iota(jnp.int32, (CHUNK, LANES), 1) < back
            p0[pl.ds(s, CHUNK, stride=step), :] = jnp.where(keep, a, b)
            p1[pl.ds(s, CHUNK, stride=step), :] = jnp.where(keep, b, c)
            return carry

        lax.fori_loop(0, inner, gather, 0, unroll=124)
        edge_ready()
        lax.fori_loop(inner, segs, gather, 0, unroll=4)
        table = table_ref[pl.ds(pl.multiple_of(side * NF, NF), NF), :]

        def transform(i, carry):
            pair = [pl.ds(pl.multiple_of((2 * i + part) * step, 8), segs) for part in range(2)]
            piece = jnp.concatenate([jnp.concatenate([p0[rows, :], p1[rows, :]], axis=1) for rows in pair]).astype(jnp.bfloat16)
            spec = lax.dot_general(table, piece, (((1,), (1,)), ((), ())), preferred_element_type=jnp.float32)
            for part in range(2):
                both = spec[:, part * segs:(part + 1) * segs]
                s0[pl.ds(2 * i + part, half_bins, stride=CHUNK + 8), :] = both[:half_bins]
                s1[pl.ds(2 * i + part, half_bins, stride=CHUNK + 8), :] = both[half_bins:]
            return carry

        lax.fori_loop(0, CHUNK // 2, transform, 0, unroll=8)

        def pack(f, carry):
            rows = pl.ds(pl.multiple_of(f * (CHUNK + 8), 8), CHUNK)
            send[slot, chunk, f] = jnp.concatenate([s0[rows, :], s1[rows, :]], axis=1).astype(jnp.bfloat16)
            return carry

        lax.fori_loop(0, half_bins, pack, 0, unroll=8)

        def launch(d, carry):
            block_copy(slot, chunk, origin, peer(ranks + half - d)).start()
            return carry

        lax.fori_loop(half + 1, ranks, launch, 0)
        recv[chunk, origin] = send[slot, chunk, pl.ds(lax.rem(me, half) * own, own)]

    load_table.wait()
    load_offsets.wait()
    load_steps.wait()

    def own_spectra(chunk, carry):
        def edge_ready():
            @pl.when((chunk == 0) & (tm < blocks - 1))
            def _():
                halo_copy(tm + 1).wait_recv()

        spectra(0, chunk, me, edge_ready)
        return carry

    lax.fori_loop(0, chunks, own_spectra, 0)

    for block in range(NP // LANES):
        row = slow_ref[:, block * LANES:(block + 1) * LANES].astype(jnp.float32)
        across = lax.broadcasted_iota(jnp.int32, (LANES, LANES), 1)
        down = lax.broadcasted_iota(jnp.int32, (LANES, LANES), 0)
        column = jnp.sum(jnp.where(across == down, jnp.broadcast_to(row, (LANES, LANES)), 0.0), axis=1, keepdims=True)
        slow[block * LANES:(block + 1) * LANES, :] = jnp.broadcast_to(column, (LANES, LANES)).astype(jnp.int32)

    def steering(step, carry):
        f, rows = step // (NP // ROWS), lax.rem(step, NP // ROWS) * ROWS
        rows = pl.multiple_of(rows, ROWS)
        kp = (slow[pl.ds(rows, ROWS), :] * (me * own + f + 1)) & (modulus - 1)
        lane = lax.broadcasted_iota(jnp.int32, (ROWS, LANES), 1)
        first = (lane // CHUNK) * chans + (lane & (CHUNK - 1))
        scale = 1.0 / math.sqrt(total)
        cos0, sin0 = turn((kp * first) & (modulus - 1))
        cos0, sin0 = cos0 * scale, sin0 * scale
        hops = jnp.where(lane == 0, CHUNK, (LANES // CHUNK) * chans)
        cosp, sinp = turn((kp * hops) & (modulus - 1))
        rc, rs, bc, bs = [jnp.broadcast_to(v[:, i:i + 1], (ROWS, LANES)) for i in (0, 1) for v in (cosp, sinp)]
        for block in range(width // LANES):
            columns = slice(block * LANES, (block + 1) * LANES)
            cos, sin = cos0, sin0
            for chunk in range(chunks):
                steer[f, chunk, pl.ds(rows, ROWS), columns] = cos.astype(jnp.bfloat16)
                steer[f, chunk, pl.ds(NP + rows, ROWS), columns] = sin.astype(jnp.bfloat16)
                cos, sin = cos * rc - sin * rs, cos * rs + sin * rc
            cos0, sin0 = cos0 * bc - sin0 * bs, cos0 * bs + sin0 * bc
        return carry

    steps = own * (NP // ROWS)

    def mirror_spectra(chunk, carry):
        lax.fori_loop(steps * chunk // (2 * chunks), steps * (chunk + 1) // (2 * chunks), steering, 0)
        signal_copy(chunk).wait_send()

        @pl.when(chunk + 2 < chunks)
        def _():
            signal_copy(chunk + 2).start()

        signal_copy(chunk).wait_recv()

        @pl.when(tm > 0)
        def _():
            edge_copy(chunk, tm - 1).start()

        def edge_ready():
            @pl.when(tm < blocks - 1)
            def _():
                edge_copy(chunk, tm + 1).wait_recv()

        spectra(1, chunk, mirror, edge_ready)
        return carry

    lax.fori_loop(0, chunks, mirror_spectra, 0)
    lax.fori_loop(steps // 2, steps, steering, 0)

    others = pl.ds(0, ranks - 1)

    def arrivals(slot, chunk):
        held = recv.at[chunk, pl.ds(0, half - 1)]
        pltpu.make_async_copy(held, held, recv_sems.at[slot, chunk]).wait()

    def add(chunk, first):
        arrivals(0, chunk)
        arrivals(1, chunk)

        def one_bin(f, carry):
            spec = recv[chunk, :, f].reshape(width, 2 * segs)
            both = jnp.dot(steer[f, chunk], spec, preferred_element_type=jnp.float32)
            real = both[:NP, :segs] - both[NP:, segs:]
            imag = both[:NP, segs:] + both[NP:, :segs]
            beam_ref[f, 0] = real if first else beam_ref[f, 0] + real
            beam_ref[f, 1] = imag if first else beam_ref[f, 1] + imag
            return carry

        lax.fori_loop(0, own, one_bin, 0, unroll=8)

    add(0, True)

    def more(chunk, carry):
        add(chunk, False)
        return carry

    lax.fori_loop(1, chunks - 1, more, 0)

    def power_copy(to):
        return pltpu.make_async_remote_copy(
            src_ref=terms.at[to],
            dst_ref=arrived.at[me],
            send_sem=power_sems.at[0],
            recv_sem=power_sems.at[1],
            device_id={"chan": to},
            device_id_type=pl.DeviceIdType.MESH,
        )

    last = chunks - 1
    rows_of_side = NP // 2
    energy[...] = jnp.zeros((rows_of_side, segs), jnp.float32)

    def half_sum(f, group, base, count):
        columns = pl.ds(pl.multiple_of(group * (width // 2), width // 2), width // 2)
        steps = [steer[f, last, pl.ds(base + part * NP, count), columns] for part in range(2)]
        spec = recv[last, pl.ds(group * half, half), f].reshape(width // 2, 2 * segs)
        turned = jnp.concatenate([-spec[:, segs:], spec[:, :segs]], axis=1)
        both = jnp.dot(jnp.concatenate(steps, axis=1), jnp.concatenate([spec, turned]), preferred_element_type=jnp.float32)
        return both[:, :segs], both[:, segs:]

    arrivals(0, last)

    def own_half(f, carry):
        real, imag = half_sum(f, side, 0, NP)
        beam_ref[f, 0] += real
        beam_ref[f, 1] += imag
        return carry

    lax.fori_loop(0, own, own_half, 0, unroll=8)
    arrivals(1, last)

    def finish_side(phase, carry):
        owners = lax.rem(side + 1 + phase, 2)
        base = pl.multiple_of(owners * rows_of_side, rows_of_side)
        rows = pl.ds(base, rows_of_side)

        def one_bin(f, acc):
            real, imag = half_sum(f, 1 - side, base, rows_of_side)
            real, imag = beam_ref[f, 0, rows, :] + real, beam_ref[f, 1, rows, :] + imag
            beam_ref[f, 0, rows, :] = real
            beam_ref[f, 1, rows, :] = imag
            energy[...] = jnp.where(f == 0, 0.0, energy[...]) + (real * real + imag * imag)
            return acc

        lax.fori_loop(0, own, one_bin, 0, unroll=8)
        mine = terms.at[pl.ds(owners * half, half)]
        mine[...] = (energy[...] * (1.0 / NF)).reshape(half, slows, segs).astype(terms.dtype)

        def power_term(d, carry):
            power_copy(peer(half - 1 - d + phase * (ranks + 1))).start()
            return carry

        lax.fori_loop(phase * (half + 1), half + phase * half, power_term, 0)
        return carry

    lax.fori_loop(0, 2, finish_side, 0)
    arrived[me] = terms[me]
    pltpu.make_async_copy(arrived.at[others], arrived.at[others], power_sems.at[1]).wait()

    def sum_up(r, acc):
        return acc + arrived[r].astype(jnp.float32)

    power_ref[...] = lax.fori_loop(0, ranks, sum_up, jnp.zeros((slows, segs), jnp.float32), unroll=16)

    def finish(chunk, carry):
        sent = recv.at[chunk, pl.ds(0, half - 1)]
        pltpu.make_async_copy(sent, sent, send_sems.at[0, chunk]).wait()
        pltpu.make_async_copy(sent, sent, send_sems.at[1, chunk]).wait()

        @pl.when(tm > 0)
        def _():
            edge_copy(chunk, tm - 1).wait_send()

        return carry

    lax.fori_loop(0, chunks, finish, 0)
    pltpu.make_async_copy(terms.at[others], terms.at[others], power_sems.at[0]).wait()

    @pl.when(tm > 0)
    def _():
        halo_copy(tm - 1).wait_send()


def fused(signal, mask, offsets, table, slow, ranks, blocks):
    chans, segs = signal.shape[0], offsets.shape[0]
    slows = NP // ranks
    term = jnp.bfloat16 if slows % 16 == 0 else jnp.float32
    own, chunks = NF // ranks, chans // CHUNK
    vmem = pl.BlockSpec(memory_space=pltpu.VMEM)
    return pl.pallas_call(
        functools.partial(fused_kernel, ranks=ranks, blocks=blocks),
        out_shape=(
            pltpu.VMEM((own, 2, NP, segs), jnp.float32),
            pltpu.VMEM((NP // ranks, segs), jnp.float32),
        ),
        in_specs=[pl.BlockSpec(memory_space=pl.ANY)] * 5,
        out_specs=(vmem, vmem),
        scratch_shapes=[
            pltpu.SMEM(offsets.shape, offsets.dtype),
            pltpu.VMEM(mask.shape, mask.dtype),
            pltpu.VMEM(table.shape, table.dtype),
            pltpu.VMEM(slow.shape, slow.dtype),
            pltpu.VMEM(signal.shape, signal.dtype),
            pltpu.VMEM((NP, LANES), jnp.int32),
            pltpu.VMEM((2, chans, signal.shape[1] + SEG), jnp.bfloat16),
        ]
        + [pltpu.VMEM((CHUNK * (segs + PAD), LANES), jnp.float32)] * 2
        + [pltpu.VMEM((NF // 2 * (CHUNK + 8), segs), jnp.float32)] * 2
        + [
            pltpu.VMEM((2, chunks, NF // 2, CHUNK, 2 * segs), jnp.bfloat16),
            pltpu.VMEM((chunks, ranks, own, CHUNK, 2 * segs), jnp.bfloat16),
            pltpu.VMEM((own, chunks, 2 * NP, ranks * CHUNK), jnp.bfloat16),
            pltpu.VMEM((NP // 2, segs), jnp.float32),
            pltpu.VMEM((ranks, slows, segs), term),
            pltpu.VMEM((ranks, slows, segs), term),
            pltpu.SemaphoreType.DMA((2, chunks)),
            pltpu.SemaphoreType.DMA((2, chunks)),
            pltpu.SemaphoreType.DMA((2,)),
            pltpu.SemaphoreType.DMA((2,)),
            pltpu.SemaphoreType.DMA((chunks,)),
            pltpu.SemaphoreType.DMA((chunks,)),
            pltpu.SemaphoreType.DMA((chunks,)),
            pltpu.SemaphoreType.DMA((chunks,)),
            pltpu.SemaphoreType.DMA((chunks,)),
            pltpu.SemaphoreType.DMA((4,)),
        ],
        compiler_params=pltpu.CompilerParams(vmem_limit_bytes=VMEM_LIMIT, collective_id=0, has_side_effects=True),
        cost_estimate=pl.CostEstimate(flops=7 << 30, bytes_accessed=8 << 20, transcendentals=0),
        name="beamform",
    )(*[pltpu.with_memory_space_constraint(x, pltpu.HBM) for x in (offsets, signal, mask, table, slow)])


def store_kernel(beam_ref, power_ref, beam_out, power_out, sems):
    bins = beam_ref.shape[0]

    def copy(f):
        return pltpu.make_async_copy(beam_ref.at[f], beam_out.at[f], sems.at[f])

    last = pltpu.make_async_copy(power_ref, power_out, sems.at[bins])
    for f in range(bins):
        copy(f).start()
    last.start()
    for f in range(bins):
        copy(f).wait()
    last.wait()


def store(beam, power):
    vmem, anywhere = pl.BlockSpec(memory_space=pltpu.VMEM), pl.BlockSpec(memory_space=pl.ANY)
    return pl.pallas_call(
        store_kernel,
        out_shape=(jax.ShapeDtypeStruct(beam.shape, beam.dtype), jax.ShapeDtypeStruct(power.shape, power.dtype)),
        in_specs=[vmem, vmem],
        out_specs=(anywhere, anywhere),
        scratch_shapes=[pltpu.SemaphoreType.DMA((beam.shape[0] + 1,))],
        cost_estimate=pl.CostEstimate(flops=0, bytes_accessed=2 * beam.size * 4, transcendentals=0),
        compiler_params=pltpu.CompilerParams(vmem_limit_bytes=8 << 20),
        name="store",
    )(*[pltpu.with_memory_space_constraint(x, pltpu.VMEM) for x in (beam, power)])


def local(signal, channel_mask, seg_offsets, slow_steps):
    ranks, blocks = lax.axis_size("chan"), lax.axis_size("tm")
    return store(*fused(signal, channel_mask[None, :], seg_offsets, make_table(), slow_steps[None, :], ranks, blocks))


def solution(mesh):
    in_specs = (P("chan", "tm"), P("chan"), P("tm"), P())
    out_specs = (P("chan", None, None, "tm"), P("chan", "tm"))
    return jax.shard_map(local, mesh=mesh, in_specs=in_specs, out_specs=out_specs, check_vma=False)
```

```python
import functools
import math

import jax
import jax.numpy as jnp
import ml_dtypes
import numpy as np
from jax import lax
from jax.experimental import pallas as pl
from jax.experimental.pallas import tpu as pltpu
from jax.sharding import PartitionSpec as P

SEG = 256
NF = 128
NP = 512
SUBSTEPS = 16
HOP = 64
LANES = 128
CHUNK = 16
ROWS = 64
PAD = 8
VMEM_LIMIT = 46 * 1024 * 1024


def make_table():
    points = np.arange(SEG)
    bins = np.arange(1, NF + 1)
    taper = 0.5 - 0.5 * np.cos(2.0 * np.pi * points / SEG)
    angle = ((bins[:, None] * points[None, :]) % SEG) * (2.0 * np.pi / SEG)
    scale = 1.0 / math.sqrt(3.0 * SEG / 8.0)
    table = np.stack([taper * np.cos(angle), -taper * np.sin(angle)]).reshape(2, 2, NF // 2, SEG) * scale
    table = table.transpose(1, 0, 2, 3).reshape(2 * NF, SEG)
    return jnp.asarray(table.astype(np.float32).astype(ml_dtypes.bfloat16))


def turn(index):
    quarter = SEG * SUBSTEPS // 4
    quadrant = (index + quarter // 2) >> 10
    x = (index - quadrant * quarter).astype(jnp.float32) * (0.5 * math.pi / quarter)
    y = x * x
    sin = x * (1.0 + y * (-1.0 / 6 + y * (1.0 / 120 + y * (-1.0 / 5040 + y * (1.0 / 362880)))))
    cos = 1.0 + y * (-0.5 + y * (1.0 / 24 + y * (-1.0 / 720 + y * (1.0 / 40320))))
    odd = (quadrant & 1) == 1
    c, d = jnp.where(odd, sin, cos), jnp.where(odd, cos, sin)
    return jnp.where(((quadrant + 1) & 2) == 2, -c, c), jnp.where((quadrant & 2) == 2, -d, d)


def fused_kernel(offsets_ref, signal_ref, channel_mask_ref, taper_ref, steps_ref, beam_ref, power_ref, offs, mask_ref, table_ref, slow_ref, x_ref, slow, held_signal, p0, p1, s0, s1, send, recv, steer, energy, terms, arrived, send_sems, recv_sems, power_sems, halo_sems, signal_sends, signal_recvs, edge_sends, edge_recvs, load_sems, small_sems, *, ranks, blocks):
    chans = signal_ref.shape[0]
    chunks = chans // CHUNK
    step = p0.shape[0] // CHUNK
    segs = step - PAD
    own = NF // ranks
    slows = NP // ranks
    width = ranks * CHUNK
    total = chans * ranks
    modulus = SEG * SUBSTEPS
    me = lax.axis_index("chan")

    tm = lax.axis_index("tm")
    half = ranks // 2
    side = me // half
    mirror = (1 - side) * half + lax.rem(me, half)
    span = signal_ref.shape[1]
    half_bins = NF // 2

    def peer(d):
        return (1 - side + d // half) % 2 * half + ((me % half) ^ (d % half))

    barrier = pltpu.get_barrier_semaphore()
    mesh_ids = pl.DeviceIdType.MESH

    def greet(d, carry):
        pl.semaphore_signal(barrier, inc=1, device_id={"chan": peer(d)}, device_id_type=mesh_ids)
        return carry

    def others_of(body):
        lax.fori_loop(0, half, body, 0, unroll=8)
        lax.fori_loop(half + 1, ranks, body, 0, unroll=min(7, half - 1))

    @pl.when(tm > 0)
    def _():
        pl.semaphore_signal(barrier, inc=1, device_id={"tm": tm - 1}, device_id_type=mesh_ids)

    @pl.when(tm < blocks - 1)
    def _():
        pl.semaphore_signal(barrier, inc=1, device_id={"tm": tm + 1}, device_id_type=mesh_ids)

    others_of(greet)

    smalls = ((channel_mask_ref, mask_ref), (taper_ref, table_ref), (offsets_ref, offs), (steps_ref, slow_ref))
    load_mask, load_table, load_offsets, load_steps = [pltpu.make_async_copy(*pair, small_sems.at[i]) for i, pair in enumerate(smalls)]
    load_mask.start()
    for chunk in range(chunks):
        rows = pl.ds(chunk * CHUNK, CHUNK)
        pltpu.make_async_copy(signal_ref.at[rows], x_ref.at[rows], load_sems.at[chunk]).start()

    load_table.start()
    load_offsets.start()
    load_steps.start()

    def load(chunk):
        rows = pl.ds(pl.multiple_of(chunk * CHUNK, CHUNK), CHUNK)
        return pltpu.make_async_copy(signal_ref.at[rows], x_ref.at[rows], load_sems.at[chunk])

    edge = SEG // LANES

    def mask_tiles(chunk, low, high):
        rows = pl.ds(pl.multiple_of(chunk * CHUNK, CHUNK), CHUNK)
        across = lax.broadcasted_iota(jnp.int32, (CHUNK, chans), 1)
        down = lax.broadcasted_iota(jnp.int32, (CHUNK, chans), 0) + chunk * CHUNK
        live = jnp.broadcast_to(mask_ref[...].astype(jnp.float32), (CHUNK, chans))
        mask = jnp.sum(jnp.where(across == down, live, 0.0), axis=1, keepdims=True)
        mask = jnp.broadcast_to(mask, (CHUNK, LANES)).astype(jnp.bfloat16)

        def one(tile, carry):
            columns = pl.ds(pl.multiple_of(tile * LANES, LANES), LANES)
            held_signal[0, rows, columns] = x_ref[rows, columns] * mask
            return carry

        lax.fori_loop(low, high, one, 0, unroll=(high - low) // 2)

    def mask_edge(chunk, carry):
        load(chunk).wait()
        mask_tiles(chunk, 0, edge)
        return carry

    def mask_rows(chunk, carry):
        mask_tiles(chunk, edge, span // LANES)
        return carry

    load_mask.wait()
    lax.fori_loop(0, chunks, mask_edge, 0)
    lax.fori_loop(0, 2, mask_rows, 0)
    pl.semaphore_wait(barrier, ranks - 1 + jnp.where(tm > 0, 1, 0) + jnp.where(tm < blocks - 1, 1, 0))

    def halo_copy(to):
        return pltpu.make_async_remote_copy(
            src_ref=held_signal.at[0, :, pl.ds(0, SEG)],
            dst_ref=held_signal.at[0, :, pl.ds(span, SEG)],
            send_sem=halo_sems.at[0],
            recv_sem=halo_sems.at[1],
            device_id={"tm": to},
            device_id_type=mesh_ids,
        )

    def signal_copy(chunk):
        rows = pl.ds(pl.multiple_of(chunk * CHUNK, CHUNK), CHUNK)
        return pltpu.make_async_remote_copy(
            src_ref=held_signal.at[0, rows, pl.ds(0, span)],
            dst_ref=held_signal.at[1, rows, pl.ds(0, span)],
            send_sem=signal_sends.at[chunk],
            recv_sem=signal_recvs.at[chunk],
            device_id={"chan": mirror},
            device_id_type=mesh_ids,
        )

    def edge_copy(chunk, to):
        rows = pl.ds(pl.multiple_of(chunk * CHUNK, CHUNK), CHUNK)
        return pltpu.make_async_remote_copy(
            src_ref=held_signal.at[1, rows, pl.ds(0, SEG)],
            dst_ref=held_signal.at[1, rows, pl.ds(span, SEG)],
            send_sem=edge_sends.at[chunk],
            recv_sem=edge_recvs.at[chunk],
            device_id={"tm": to},
            device_id_type=mesh_ids,
        )

    def send_signal(chunk, carry):
        signal_copy(chunk).start()
        return carry

    @pl.when(tm > 0)
    def _():
        halo_copy(tm - 1).start()

    lax.fori_loop(0, 2, send_signal, 0)
    lax.fori_loop(2, chunks, mask_rows, 0)

    @pl.when(tm == blocks - 1)
    def _():
        held_signal[:, :, span:] = jnp.zeros((2, chans, SEG), jnp.bfloat16)

    def block_copy(slot, chunk, origin, to):
        return pltpu.make_async_remote_copy(
            src_ref=send.at[slot, chunk, pl.ds(lax.rem(to, half) * own, own)],
            dst_ref=recv.at[chunk, origin],
            send_sem=send_sems.at[slot, chunk],
            recv_sem=recv_sems.at[slot, chunk],
            device_id={"chan": to},
            device_id_type=mesh_ids,
        )

    inner = 2 * ((span - 3 * LANES) // LANES + 1)

    def spectra(slot, chunk, origin, edge_ready):
        top = pl.multiple_of(chunk * CHUNK, CHUNK)

        def gather(s, carry):
            start = pl.multiple_of((s // 2) * LANES, LANES)
            back = LANES - (offs[s] - start)
            tiles = held_signal[slot, pl.ds(top, CHUNK), pl.ds(start, 3 * LANES)].astype(jnp.float32)
            a, b, c = [pltpu.roll(tiles[:, i * LANES:(i + 1) * LANES], back, 1) for i in range(3)]
            keep = lax.broadcasted_iota(jnp.int32, (CHUNK, LANES), 1) < back
            p0[pl.ds(s, CHUNK, stride=step), :] = jnp.where(keep, a, b)
            p1[pl.ds(s, CHUNK, stride=step), :] = jnp.where(keep, b, c)
            return carry

        lax.fori_loop(0, inner, gather, 0, unroll=124)
        edge_ready()
        lax.fori_loop(inner, segs, gather, 0, unroll=4)
        table = table_ref[pl.ds(pl.multiple_of(side * NF, NF), NF), :]

        def transform(i, carry):
            pair = [pl.ds(pl.multiple_of((2 * i + part) * step, 8), segs) for part in range(2)]
            piece = jnp.concatenate([jnp.concatenate([p0[rows, :], p1[rows, :]], axis=1) for rows in pair]).astype(jnp.bfloat16)
            spec = lax.dot_general(table, piece, (((1,), (1,)), ((), ())), preferred_element_type=jnp.float32)
            for part in range(2):
                both = spec[:, part * segs:(part + 1) * segs]
                s0[pl.ds(2 * i + part, half_bins, stride=CHUNK + 8), :] = both[:half_bins]
                s1[pl.ds(2 * i + part, half_bins, stride=CHUNK + 8), :] = both[half_bins:]
            return carry

        lax.fori_loop(0, CHUNK // 2, transform, 0, unroll=8)

        def pack(f, carry):
            rows = pl.ds(pl.multiple_of(f * (CHUNK + 8), 8), CHUNK)
            send[slot, chunk, f] = jnp.concatenate([s0[rows, :], s1[rows, :]], axis=1).astype(jnp.bfloat16)
            return carry

        lax.fori_loop(0, half_bins, pack, 0, unroll=8)

        def launch(d, carry):
            block_copy(slot, chunk, origin, peer(ranks + half - d)).start()
            return carry

        lax.fori_loop(half + 1, ranks, launch, 0)
        recv[chunk, origin] = send[slot, chunk, pl.ds(lax.rem(me, half) * own, own)]

    load_table.wait()
    load_offsets.wait()
    load_steps.wait()

    def own_spectra(chunk, carry):
        def edge_ready():
            @pl.when((chunk == 0) & (tm < blocks - 1))
            def _():
                halo_copy(tm + 1).wait_recv()

        spectra(0, chunk, me, edge_ready)
        return carry

    lax.fori_loop(0, chunks, own_spectra, 0)

    for block in range(NP // LANES):
        row = slow_ref[:, block * LANES:(block + 1) * LANES].astype(jnp.float32)
        across = lax.broadcasted_iota(jnp.int32, (LANES, LANES), 1)
        down = lax.broadcasted_iota(jnp.int32, (LANES, LANES), 0)
        column = jnp.sum(jnp.where(across == down, jnp.broadcast_to(row, (LANES, LANES)), 0.0), axis=1, keepdims=True)
        slow[block * LANES:(block + 1) * LANES, :] = jnp.broadcast_to(column, (LANES, LANES)).astype(jnp.int32)

    def steering(step, carry):
        f, rows = step // (NP // ROWS), lax.rem(step, NP // ROWS) * ROWS
        rows = pl.multiple_of(rows, ROWS)
        kp = (slow[pl.ds(rows, ROWS), :] * (me * own + f + 1)) & (modulus - 1)
        lane = lax.broadcasted_iota(jnp.int32, (ROWS, LANES), 1)
        first = (lane // CHUNK) * chans + (lane & (CHUNK - 1))
        scale = 1.0 / math.sqrt(total)
        cos0, sin0 = turn((kp * first) & (modulus - 1))
        cos0, sin0 = cos0 * scale, sin0 * scale
        hops = jnp.where(lane == 0, CHUNK, (LANES // CHUNK) * chans)
        cosp, sinp = turn((kp * hops) & (modulus - 1))
        rc, rs, bc, bs = [jnp.broadcast_to(v[:, i:i + 1], (ROWS, LANES)) for i in (0, 1) for v in (cosp, sinp)]
        for block in range(width // LANES):
            columns = slice(block * LANES, (block + 1) * LANES)
            cos, sin = cos0, sin0
            for chunk in range(chunks):
                steer[f, chunk, pl.ds(rows, ROWS), columns] = cos.astype(jnp.bfloat16)
                steer[f, chunk, pl.ds(NP + rows, ROWS), columns] = sin.astype(jnp.bfloat16)
                cos, sin = cos * rc - sin * rs, cos * rs + sin * rc
            cos0, sin0 = cos0 * bc - sin0 * bs, cos0 * bs + sin0 * bc
        return carry

    steps = own * (NP // ROWS)

    def mirror_spectra(chunk, carry):
        lax.fori_loop(steps * chunk // (2 * chunks), steps * (chunk + 1) // (2 * chunks), steering, 0)
        signal_copy(chunk).wait_send()

        @pl.when(chunk + 2 < chunks)
        def _():
            signal_copy(chunk + 2).start()

        signal_copy(chunk).wait_recv()

        @pl.when(tm > 0)
        def _():
            edge_copy(chunk, tm - 1).start()

        def edge_ready():
            @pl.when(tm < blocks - 1)
            def _():
                edge_copy(chunk, tm + 1).wait_recv()

        spectra(1, chunk, mirror, edge_ready)
        return carry

    lax.fori_loop(0, chunks, mirror_spectra, 0)
    lax.fori_loop(steps // 2, steps, steering, 0)

    others = pl.ds(0, ranks - 1)

    def arrivals(slot, chunk):
        held = recv.at[chunk, pl.ds(0, half - 1)]
        pltpu.make_async_copy(held, held, recv_sems.at[slot, chunk]).wait()

    def add(chunk, first):
        arrivals(0, chunk)
        arrivals(1, chunk)

        def one_bin(f, carry):
            spec = recv[chunk, :, f].reshape(width, 2 * segs)
            both = jnp.dot(steer[f, chunk], spec, preferred_element_type=jnp.float32)
            real = both[:NP, :segs] - both[NP:, segs:]
            imag = both[:NP, segs:] + both[NP:, :segs]
            beam_ref[f, 0] = real if first else beam_ref[f, 0] + real
            beam_ref[f, 1] = imag if first else beam_ref[f, 1] + imag
            return carry

        lax.fori_loop(0, own, one_bin, 0, unroll=8)

    add(0, True)

    def more(chunk, carry):
        add(chunk, False)
        return carry

    lax.fori_loop(1, chunks - 1, more, 0)

    def power_copy(to):
        return pltpu.make_async_remote_copy(
            src_ref=terms.at[to],
            dst_ref=arrived.at[me],
            send_sem=power_sems.at[0],
            recv_sem=power_sems.at[1],
            device_id={"chan": to},
            device_id_type=pl.DeviceIdType.MESH,
        )

    last = chunks - 1
    rows_of_side = NP // 2
    energy[...] = jnp.zeros((rows_of_side, segs), jnp.float32)

    def half_sum(f, group, base, count):
        columns = pl.ds(pl.multiple_of(group * (width // 2), width // 2), width // 2)
        steps = [steer[f, last, pl.ds(base + part * NP, count), columns] for part in range(2)]
        spec = recv[last, pl.ds(group * half, half), f].reshape(width // 2, 2 * segs)
        turned = jnp.concatenate([-spec[:, segs:], spec[:, :segs]], axis=1)
        both = jnp.dot(jnp.concatenate(steps, axis=1), jnp.concatenate([spec, turned]), preferred_element_type=jnp.float32)
        return both[:, :segs], both[:, segs:]

    arrivals(0, last)

    def own_half(f, carry):
        real, imag = half_sum(f, side, 0, NP)
        beam_ref[f, 0] += real
        beam_ref[f, 1] += imag
        return carry

    lax.fori_loop(0, own, own_half, 0, unroll=8)
    arrivals(1, last)

    def finish_side(phase, carry):
        owners = lax.rem(side + 1 + phase, 2)
        base = pl.multiple_of(owners * rows_of_side, rows_of_side)
        rows = pl.ds(base, rows_of_side)

        def one_bin(f, acc):
            real, imag = half_sum(f, 1 - side, base, rows_of_side)
            real, imag = beam_ref[f, 0, rows, :] + real, beam_ref[f, 1, rows, :] + imag
            beam_ref[f, 0, rows, :] = real
            beam_ref[f, 1, rows, :] = imag
            energy[...] = jnp.where(f == 0, 0.0, energy[...]) + (real * real + imag * imag)
            return acc

        lax.fori_loop(0, own, one_bin, 0, unroll=8)
        mine = terms.at[pl.ds(owners * half, half)]
        mine[...] = (energy[...] * (1.0 / NF)).reshape(half, slows, segs).astype(terms.dtype)

        def power_term(d, carry):
            power_copy(peer(half - 1 - d + phase * (ranks + 1))).start()
            return carry

        lax.fori_loop(phase * (half + 1), half + phase * half, power_term, 0)
        return carry

    lax.fori_loop(0, 2, finish_side, 0)
    arrived[me] = terms[me]

    def finish(chunk, carry):
        sent = recv.at[chunk, pl.ds(0, half - 1)]
        pltpu.make_async_copy(sent, sent, send_sems.at[0, chunk]).wait()
        pltpu.make_async_copy(sent, sent, send_sems.at[1, chunk]).wait()

        @pl.when(tm > 0)
        def _():
            edge_copy(chunk, tm - 1).wait_send()

        return carry

    lax.fori_loop(0, chunks, finish, 0)

    @pl.when(tm > 0)
    def _():
        halo_copy(tm - 1).wait_send()

    pltpu.make_async_copy(arrived.at[others], arrived.at[others], power_sems.at[1]).wait()

    def sum_up(r, acc):
        return acc + arrived[r].astype(jnp.float32)

    power_ref[...] = lax.fori_loop(0, ranks, sum_up, jnp.zeros((slows, segs), jnp.float32), unroll=16)

    pltpu.make_async_copy(terms.at[others], terms.at[others], power_sems.at[0]).wait()


def fused(signal, mask, offsets, table, slow, ranks, blocks):
    chans, segs = signal.shape[0], offsets.shape[0]
    slows = NP // ranks
    term = jnp.bfloat16 if slows % 16 == 0 else jnp.float32
    own, chunks = NF // ranks, chans // CHUNK
    vmem = pl.BlockSpec(memory_space=pltpu.VMEM)
    return pl.pallas_call(
        functools.partial(fused_kernel, ranks=ranks, blocks=blocks),
        out_shape=(
            pltpu.VMEM((own, 2, NP, segs), jnp.float32),
            pltpu.VMEM((NP // ranks, segs), jnp.float32),
        ),
        in_specs=[pl.BlockSpec(memory_space=pl.ANY)] * 5,
        out_specs=(vmem, vmem),
        scratch_shapes=[
            pltpu.SMEM(offsets.shape, offsets.dtype),
            pltpu.VMEM(mask.shape, mask.dtype),
            pltpu.VMEM(table.shape, table.dtype),
            pltpu.VMEM(slow.shape, slow.dtype),
            pltpu.VMEM(signal.shape, signal.dtype),
            pltpu.VMEM((NP, LANES), jnp.int32),
            pltpu.VMEM((2, chans, signal.shape[1] + SEG), jnp.bfloat16),
        ]
        + [pltpu.VMEM((CHUNK * (segs + PAD), LANES), jnp.float32)] * 2
        + [pltpu.VMEM((NF // 2 * (CHUNK + 8), segs), jnp.float32)] * 2
        + [
            pltpu.VMEM((2, chunks, NF // 2, CHUNK, 2 * segs), jnp.bfloat16),
            pltpu.VMEM((chunks, ranks, own, CHUNK, 2 * segs), jnp.bfloat16),
            pltpu.VMEM((own, chunks, 2 * NP, ranks * CHUNK), jnp.bfloat16),
            pltpu.VMEM((NP // 2, segs), jnp.float32),
            pltpu.VMEM((ranks, slows, segs), term),
            pltpu.VMEM((ranks, slows, segs), term),
            pltpu.SemaphoreType.DMA((2, chunks)),
            pltpu.SemaphoreType.DMA((2, chunks)),
            pltpu.SemaphoreType.DMA((2,)),
            pltpu.SemaphoreType.DMA((2,)),
            pltpu.SemaphoreType.DMA((chunks,)),
            pltpu.SemaphoreType.DMA((chunks,)),
            pltpu.SemaphoreType.DMA((chunks,)),
            pltpu.SemaphoreType.DMA((chunks,)),
            pltpu.SemaphoreType.DMA((chunks,)),
            pltpu.SemaphoreType.DMA((4,)),
        ],
        compiler_params=pltpu.CompilerParams(vmem_limit_bytes=VMEM_LIMIT, collective_id=0, has_side_effects=True),
        cost_estimate=pl.CostEstimate(flops=7 << 30, bytes_accessed=8 << 20, transcendentals=0),
        name="beamform",
    )(*[pltpu.with_memory_space_constraint(x, pltpu.HBM) for x in (offsets, signal, mask, table, slow)])


def store_kernel(beam_ref, power_ref, beam_out, power_out, sems):
    bins = beam_ref.shape[0]

    def copy(f):
        return pltpu.make_async_copy(beam_ref.at[f], beam_out.at[f], sems.at[f])

    last = pltpu.make_async_copy(power_ref, power_out, sems.at[bins])
    for f in range(bins):
        copy(f).start()
    last.start()
    for f in range(bins):
        copy(f).wait()
    last.wait()


def store(beam, power):
    vmem, anywhere = pl.BlockSpec(memory_space=pltpu.VMEM), pl.BlockSpec(memory_space=pl.ANY)
    return pl.pallas_call(
        store_kernel,
        out_shape=(jax.ShapeDtypeStruct(beam.shape, beam.dtype), jax.ShapeDtypeStruct(power.shape, power.dtype)),
        in_specs=[vmem, vmem],
        out_specs=(anywhere, anywhere),
        scratch_shapes=[pltpu.SemaphoreType.DMA((beam.shape[0] + 1,))],
        cost_estimate=pl.CostEstimate(flops=0, bytes_accessed=2 * beam.size * 4, transcendentals=0),
        compiler_params=pltpu.CompilerParams(vmem_limit_bytes=8 << 20),
        name="store",
    )(*[pltpu.with_memory_space_constraint(x, pltpu.VMEM) for x in (beam, power)])


def local(signal, channel_mask, seg_offsets, slow_steps):
    ranks, blocks = lax.axis_size("chan"), lax.axis_size("tm")
    return store(*fused(signal, channel_mask[None, :], seg_offsets, make_table(), slow_steps[None, :], ranks, blocks))


def solution(mesh):
    in_specs = (P("chan", "tm"), P("chan"), P("tm"), P())
    out_specs = (P("chan", None, None, "tm"), P("chan", "tm"))
    return jax.shard_map(local, mesh=mesh, in_specs=in_specs, out_specs=out_specs, check_vma=False)
```

```python
import functools
import math

import jax
import jax.numpy as jnp
import ml_dtypes
import numpy as np
from jax import lax
from jax.experimental import pallas as pl
from jax.experimental.pallas import tpu as pltpu
from jax.sharding import PartitionSpec as P

SEG = 256
NF = 128
NP = 512
SUBSTEPS = 16
HOP = 64
LANES = 128
CHUNK = 16
ROWS = 64
PAD = 8
VMEM_LIMIT = 46 * 1024 * 1024


def make_table():
    points = np.arange(SEG)
    bins = np.arange(1, NF + 1)
    taper = 0.5 - 0.5 * np.cos(2.0 * np.pi * points / SEG)
    angle = ((bins[:, None] * points[None, :]) % SEG) * (2.0 * np.pi / SEG)
    scale = 1.0 / math.sqrt(3.0 * SEG / 8.0)
    table = np.stack([taper * np.cos(angle), -taper * np.sin(angle)]).reshape(2, 2, NF // 2, SEG) * scale
    table = table.transpose(1, 0, 2, 3).reshape(2 * NF, SEG)
    return jnp.asarray(table.astype(np.float32).astype(ml_dtypes.bfloat16))


def turn(index):
    quarter = SEG * SUBSTEPS // 4
    quadrant = (index + quarter // 2) >> 10
    x = (index - quadrant * quarter).astype(jnp.float32) * (0.5 * math.pi / quarter)
    y = x * x
    sin = x * (1.0 + y * (-1.0 / 6 + y * (1.0 / 120 + y * (-1.0 / 5040 + y * (1.0 / 362880)))))
    cos = 1.0 + y * (-0.5 + y * (1.0 / 24 + y * (-1.0 / 720 + y * (1.0 / 40320))))
    odd = (quadrant & 1) == 1
    c, d = jnp.where(odd, sin, cos), jnp.where(odd, cos, sin)
    return jnp.where(((quadrant + 1) & 2) == 2, -c, c), jnp.where((quadrant & 2) == 2, -d, d)


def fused_kernel(offsets_ref, signal_ref, channel_mask_ref, taper_ref, steps_ref, beam_ref, power_ref, offs, mask_ref, table_ref, slow_ref, x_ref, slow, held_signal, p0, p1, s0, s1, send, recv, steer, energy, terms, arrived, send_sems, recv_sems, power_sems, halo_sems, signal_sends, signal_recvs, edge_sends, edge_recvs, load_sems, small_sems, *, ranks, blocks):
    chans = signal_ref.shape[0]
    chunks = chans // CHUNK
    step = p0.shape[0] // CHUNK
    segs = step - PAD
    own = NF // ranks
    slows = NP // ranks
    width = ranks * CHUNK
    total = chans * ranks
    modulus = SEG * SUBSTEPS
    me = lax.axis_index("chan")

    tm = lax.axis_index("tm")
    half = ranks // 2
    side = me // half
    mirror = (1 - side) * half + lax.rem(me, half)
    span = signal_ref.shape[1]
    half_bins = NF // 2

    def peer(d):
        return (1 - side + d // half) % 2 * half + ((me % half) ^ (d % half))

    barrier = pltpu.get_barrier_semaphore()
    mesh_ids = pl.DeviceIdType.MESH

    def greet(d, carry):
        pl.semaphore_signal(barrier, inc=1, device_id={"chan": peer(d)}, device_id_type=mesh_ids)
        return carry

    def others_of(body):
        lax.fori_loop(0, half, body, 0, unroll=8)
        lax.fori_loop(half + 1, ranks, body, 0, unroll=min(7, half - 1))

    @pl.when(tm > 0)
    def _():
        pl.semaphore_signal(barrier, inc=1, device_id={"tm": tm - 1}, device_id_type=mesh_ids)

    @pl.when(tm < blocks - 1)
    def _():
        pl.semaphore_signal(barrier, inc=1, device_id={"tm": tm + 1}, device_id_type=mesh_ids)

    others_of(greet)

    smalls = ((channel_mask_ref, mask_ref), (taper_ref, table_ref), (offsets_ref, offs), (steps_ref, slow_ref))
    load_mask, load_table, load_offsets, load_steps = [pltpu.make_async_copy(*pair, small_sems.at[i]) for i, pair in enumerate(smalls)]
    load_mask.start()
    for chunk in range(chunks):
        rows = pl.ds(chunk * CHUNK, CHUNK)
        pltpu.make_async_copy(signal_ref.at[rows], x_ref.at[rows], load_sems.at[chunk]).start()

    load_table.start()
    load_offsets.start()
    load_steps.start()

    def load(chunk):
        rows = pl.ds(pl.multiple_of(chunk * CHUNK, CHUNK), CHUNK)
        return pltpu.make_async_copy(signal_ref.at[rows], x_ref.at[rows], load_sems.at[chunk])

    edge = SEG // LANES

    def mask_tiles(chunk, low, high):
        rows = pl.ds(pl.multiple_of(chunk * CHUNK, CHUNK), CHUNK)
        across = lax.broadcasted_iota(jnp.int32, (CHUNK, chans), 1)
        down = lax.broadcasted_iota(jnp.int32, (CHUNK, chans), 0) + chunk * CHUNK
        live = jnp.broadcast_to(mask_ref[...].astype(jnp.float32), (CHUNK, chans))
        mask = jnp.sum(jnp.where(across == down, live, 0.0), axis=1, keepdims=True)
        mask = jnp.broadcast_to(mask, (CHUNK, LANES)).astype(jnp.bfloat16)

        def one(tile, carry):
            columns = pl.ds(pl.multiple_of(tile * LANES, LANES), LANES)
            held_signal[0, rows, columns] = x_ref[rows, columns] * mask
            return carry

        lax.fori_loop(low, high, one, 0, unroll=(high - low) // 2)

    def mask_edge(chunk, carry):
        load(chunk).wait()
        mask_tiles(chunk, 0, edge)
        return carry

    def mask_rows(chunk, carry):
        mask_tiles(chunk, edge, span // LANES)
        return carry

    load_mask.wait()
    lax.fori_loop(0, chunks, mask_edge, 0)
    lax.fori_loop(0, 2, mask_rows, 0)
    pl.semaphore_wait(barrier, ranks - 1 + jnp.where(tm > 0, 1, 0) + jnp.where(tm < blocks - 1, 1, 0))

    def halo_copy(to):
        return pltpu.make_async_remote_copy(
            src_ref=held_signal.at[0, :, pl.ds(0, SEG)],
            dst_ref=held_signal.at[0, :, pl.ds(span, SEG)],
            send_sem=halo_sems.at[0],
            recv_sem=halo_sems.at[1],
            device_id={"tm": to},
            device_id_type=mesh_ids,
        )

    def signal_copy(chunk):
        rows = pl.ds(pl.multiple_of(chunk * CHUNK, CHUNK), CHUNK)
        return pltpu.make_async_remote_copy(
            src_ref=held_signal.at[0, rows, pl.ds(0, span)],
            dst_ref=held_signal.at[1, rows, pl.ds(0, span)],
            send_sem=signal_sends.at[chunk],
            recv_sem=signal_recvs.at[chunk],
            device_id={"chan": mirror},
            device_id_type=mesh_ids,
        )

    def edge_copy(chunk, to):
        rows = pl.ds(pl.multiple_of(chunk * CHUNK, CHUNK), CHUNK)
        return pltpu.make_async_remote_copy(
            src_ref=held_signal.at[1, rows, pl.ds(0, SEG)],
            dst_ref=held_signal.at[1, rows, pl.ds(span, SEG)],
            send_sem=edge_sends.at[chunk],
            recv_sem=edge_recvs.at[chunk],
            device_id={"tm": to},
            device_id_type=mesh_ids,
        )

    def send_signal(chunk, carry):
        signal_copy(chunk).start()
        return carry

    @pl.when(tm > 0)
    def _():
        halo_copy(tm - 1).start()

    lax.fori_loop(0, 2, send_signal, 0)
    lax.fori_loop(2, chunks, mask_rows, 0)

    @pl.when(tm == blocks - 1)
    def _():
        held_signal[:, :, span:] = jnp.zeros((2, chans, SEG), jnp.bfloat16)

    def block_copy(slot, chunk, origin, to):
        return pltpu.make_async_remote_copy(
            src_ref=send.at[slot, chunk, pl.ds(lax.rem(to, half) * own, own)],
            dst_ref=recv.at[chunk, origin],
            send_sem=send_sems.at[slot, chunk],
            recv_sem=recv_sems.at[slot, chunk],
            device_id={"chan": to},
            device_id_type=mesh_ids,
        )

    inner = 2 * ((span - 3 * LANES) // LANES + 1)

    def spectra(slot, chunk, origin, edge_ready):
        top = pl.multiple_of(chunk * CHUNK, CHUNK)

        def gather(s, carry):
            start = pl.multiple_of((s // 2) * LANES, LANES)
            back = LANES - (offs[s] - start)
            tiles = held_signal[slot, pl.ds(top, CHUNK), pl.ds(start, 3 * LANES)].astype(jnp.float32)
            a, b, c = [pltpu.roll(tiles[:, i * LANES:(i + 1) * LANES], back, 1) for i in range(3)]
            keep = lax.broadcasted_iota(jnp.int32, (CHUNK, LANES), 1) < back
            p0[pl.ds(s, CHUNK, stride=step), :] = jnp.where(keep, a, b)
            p1[pl.ds(s, CHUNK, stride=step), :] = jnp.where(keep, b, c)
            return carry

        lax.fori_loop(0, inner, gather, 0, unroll=124)
        edge_ready()
        lax.fori_loop(inner, segs, gather, 0, unroll=4)
        table = table_ref[pl.ds(pl.multiple_of(side * NF, NF), NF), :]

        def transform(i, carry):
            pair = [pl.ds(pl.multiple_of((2 * i + part) * step, 8), segs) for part in range(2)]
            piece = jnp.concatenate([jnp.concatenate([p0[rows, :], p1[rows, :]], axis=1) for rows in pair]).astype(jnp.bfloat16)
            spec = lax.dot_general(table, piece, (((1,), (1,)), ((), ())), preferred_element_type=jnp.float32)
            for part in range(2):
                both = spec[:, part * segs:(part + 1) * segs]
                s0[pl.ds(2 * i + part, half_bins, stride=CHUNK + 8), :] = both[:half_bins]
                s1[pl.ds(2 * i + part, half_bins, stride=CHUNK + 8), :] = both[half_bins:]
            return carry

        lax.fori_loop(0, CHUNK // 2, transform, 0, unroll=8)

        def pack(f, carry):
            rows = pl.ds(pl.multiple_of(f * (CHUNK + 8), 8), CHUNK)
            send[slot, chunk, f] = jnp.concatenate([s0[rows, :], s1[rows, :]], axis=1).astype(jnp.bfloat16)
            return carry

        lax.fori_loop(0, half_bins, pack, 0, unroll=8)

        def launch(d, carry):
            block_copy(slot, chunk, origin, peer(ranks + half - d)).start()
            return carry

        lax.fori_loop(half + 1, ranks, launch, 0)
        recv[chunk, origin] = send[slot, chunk, pl.ds(lax.rem(me, half) * own, own)]

    load_table.wait()
    load_offsets.wait()
    load_steps.wait()

    def own_spectra(chunk, carry):
        def edge_ready():
            @pl.when((chunk == 0) & (tm < blocks - 1))
            def _():
                halo_copy(tm + 1).wait_recv()

        spectra(0, chunk, me, edge_ready)
        return carry

    lax.fori_loop(0, chunks, own_spectra, 0)

    for block in range(NP // LANES):
        row = slow_ref[:, block * LANES:(block + 1) * LANES].astype(jnp.float32)
        across = lax.broadcasted_iota(jnp.int32, (LANES, LANES), 1)
        down = lax.broadcasted_iota(jnp.int32, (LANES, LANES), 0)
        column = jnp.sum(jnp.where(across == down, jnp.broadcast_to(row, (LANES, LANES)), 0.0), axis=1, keepdims=True)
        slow[block * LANES:(block + 1) * LANES, :] = jnp.broadcast_to(column, (LANES, LANES)).astype(jnp.int32)

    def steering(step, carry):
        f, rows = step // (NP // ROWS), lax.rem(step, NP // ROWS) * ROWS
        rows = pl.multiple_of(rows, ROWS)
        kp = (slow[pl.ds(rows, ROWS), :] * (me * own + f + 1)) & (modulus - 1)
        lane = lax.broadcasted_iota(jnp.int32, (ROWS, LANES), 1)
        first = (lane // CHUNK) * chans + (lane & (CHUNK - 1))
        scale = 1.0 / math.sqrt(total)
        cos0, sin0 = turn((kp * first) & (modulus - 1))
        cos0, sin0 = cos0 * scale, sin0 * scale
        hops = jnp.where(lane == 0, CHUNK, (LANES // CHUNK) * chans)
        cosp, sinp = turn((kp * hops) & (modulus - 1))
        rc, rs, bc, bs = [jnp.broadcast_to(v[:, i:i + 1], (ROWS, LANES)) for i in (0, 1) for v in (cosp, sinp)]
        for block in range(width // LANES):
            columns = slice(block * LANES, (block + 1) * LANES)
            cos, sin = cos0, sin0
            for chunk in range(chunks):
                steer[f, chunk, pl.ds(rows, ROWS), columns] = cos.astype(jnp.bfloat16)
                steer[f, chunk, pl.ds(NP + rows, ROWS), columns] = sin.astype(jnp.bfloat16)
                cos, sin = cos * rc - sin * rs, cos * rs + sin * rc
            cos0, sin0 = cos0 * bc - sin0 * bs, cos0 * bs + sin0 * bc
        return carry

    steps = own * (NP // ROWS)

    def mirror_spectra(chunk, carry):
        lax.fori_loop(steps * chunk // (2 * chunks), steps * (chunk + 1) // (2 * chunks), steering, 0)
        signal_copy(chunk).wait_send()

        @pl.when(chunk + 2 < chunks)
        def _():
            signal_copy(chunk + 2).start()

        signal_copy(chunk).wait_recv()

        @pl.when(tm > 0)
        def _():
            edge_copy(chunk, tm - 1).start()

        def edge_ready():
            @pl.when(tm < blocks - 1)
            def _():
                edge_copy(chunk, tm + 1).wait_recv()

        spectra(1, chunk, mirror, edge_ready)
        return carry

    lax.fori_loop(0, chunks, mirror_spectra, 0)
    lax.fori_loop(steps // 2, steps, steering, 0)

    others = pl.ds(0, ranks - 1)

    def arrivals(slot, chunk):
        held = recv.at[chunk, pl.ds(0, half - 1)]
        pltpu.make_async_copy(held, held, recv_sems.at[slot, chunk]).wait()

    def add(chunk, first):
        arrivals(0, chunk)
        arrivals(1, chunk)

        def one_bin(f, carry):
            spec = recv[chunk, :, f].reshape(width, 2 * segs)
            both = jnp.dot(steer[f, chunk], spec, preferred_element_type=jnp.float32)
            real = both[:NP, :segs] - both[NP:, segs:]
            imag = both[:NP, segs:] + both[NP:, :segs]
            beam_ref[f, 0] = real if first else beam_ref[f, 0] + real
            beam_ref[f, 1] = imag if first else beam_ref[f, 1] + imag
            return carry

        lax.fori_loop(0, own, one_bin, 0, unroll=8)

    add(0, True)

    def more(chunk, carry):
        add(chunk, False)
        return carry

    lax.fori_loop(1, chunks - 2, more, 0)
    last = chunks - 1

    def half_sum(f, group, base, count):
        columns = pl.ds(pl.multiple_of(group * (width // 2), width // 2), width // 2)
        steps = [steer[f, last, pl.ds(base + part * NP, count), columns] for part in range(2)]
        spec = recv[last, pl.ds(group * half, half), f].reshape(width // 2, 2 * segs)
        turned = jnp.concatenate([-spec[:, segs:], spec[:, :segs]], axis=1)
        both = jnp.dot(jnp.concatenate(steps, axis=1), jnp.concatenate([spec, turned]), preferred_element_type=jnp.float32)
        return both[:, :segs], both[:, segs:]

    arrivals(0, last)

    def own_half(f, carry):
        real, imag = half_sum(f, side, 0, NP)
        beam_ref[f, 0] += real
        beam_ref[f, 1] += imag
        return carry

    lax.fori_loop(0, own, own_half, 0, unroll=8)
    add(chunks - 2, False)

    def power_copy(to):
        return pltpu.make_async_remote_copy(
            src_ref=terms.at[to],
            dst_ref=arrived.at[me],
            send_sem=power_sems.at[0],
            recv_sem=power_sems.at[1],
            device_id={"chan": to},
            device_id_type=pl.DeviceIdType.MESH,
        )

    rows_of_side = NP // 2
    energy[...] = jnp.zeros((rows_of_side, segs), jnp.float32)

    arrivals(1, last)

    def finish_side(phase, carry):
        owners = lax.rem(side + 1 + phase, 2)
        base = pl.multiple_of(owners * rows_of_side, rows_of_side)
        rows = pl.ds(base, rows_of_side)

        def one_bin(f, acc):
            real, imag = half_sum(f, 1 - side, base, rows_of_side)
            real, imag = beam_ref[f, 0, rows, :] + real, beam_ref[f, 1, rows, :] + imag
            beam_ref[f, 0, rows, :] = real
            beam_ref[f, 1, rows, :] = imag
            energy[...] = jnp.where(f == 0, 0.0, energy[...]) + (real * real + imag * imag)
            return acc

        lax.fori_loop(0, own, one_bin, 0, unroll=8)
        mine = terms.at[pl.ds(owners * half, half)]
        mine[...] = (energy[...] * (1.0 / NF)).reshape(half, slows, segs).astype(terms.dtype)

        def power_term(d, carry):
            power_copy(peer(half - 1 - d + phase * (ranks + 1))).start()
            return carry

        lax.fori_loop(phase * (half + 1), half + phase * half, power_term, 0)
        return carry

    lax.fori_loop(0, 2, finish_side, 0)
    arrived[me] = terms[me]

    def finish(chunk, carry):
        sent = recv.at[chunk, pl.ds(0, half - 1)]
        pltpu.make_async_copy(sent, sent, send_sems.at[0, chunk]).wait()
        pltpu.make_async_copy(sent, sent, send_sems.at[1, chunk]).wait()

        @pl.when(tm > 0)
        def _():
            edge_copy(chunk, tm - 1).wait_send()

        return carry

    lax.fori_loop(0, chunks, finish, 0)

    @pl.when(tm > 0)
    def _():
        halo_copy(tm - 1).wait_send()

    pltpu.make_async_copy(arrived.at[others], arrived.at[others], power_sems.at[1]).wait()

    def sum_up(r, acc):
        return acc + arrived[r].astype(jnp.float32)

    power_ref[...] = lax.fori_loop(0, ranks, sum_up, jnp.zeros((slows, segs), jnp.float32), unroll=16)

    pltpu.make_async_copy(terms.at[others], terms.at[others], power_sems.at[0]).wait()


def fused(signal, mask, offsets, table, slow, ranks, blocks):
    chans, segs = signal.shape[0], offsets.shape[0]
    slows = NP // ranks
    term = jnp.bfloat16 if slows % 16 == 0 else jnp.float32
    own, chunks = NF // ranks, chans // CHUNK
    vmem = pl.BlockSpec(memory_space=pltpu.VMEM)
    return pl.pallas_call(
        functools.partial(fused_kernel, ranks=ranks, blocks=blocks),
        out_shape=(
            pltpu.VMEM((own, 2, NP, segs), jnp.float32),
            pltpu.VMEM((NP // ranks, segs), jnp.float32),
        ),
        in_specs=[pl.BlockSpec(memory_space=pl.ANY)] * 5,
        out_specs=(vmem, vmem),
        scratch_shapes=[
            pltpu.SMEM(offsets.shape, offsets.dtype),
            pltpu.VMEM(mask.shape, mask.dtype),
            pltpu.VMEM(table.shape, table.dtype),
            pltpu.VMEM(slow.shape, slow.dtype),
            pltpu.VMEM(signal.shape, signal.dtype),
            pltpu.VMEM((NP, LANES), jnp.int32),
            pltpu.VMEM((2, chans, signal.shape[1] + SEG), jnp.bfloat16),
        ]
        + [pltpu.VMEM((CHUNK * (segs + PAD), LANES), jnp.float32)] * 2
        + [pltpu.VMEM((NF // 2 * (CHUNK + 8), segs), jnp.float32)] * 2
        + [
            pltpu.VMEM((2, chunks, NF // 2, CHUNK, 2 * segs), jnp.bfloat16),
            pltpu.VMEM((chunks, ranks, own, CHUNK, 2 * segs), jnp.bfloat16),
            pltpu.VMEM((own, chunks, 2 * NP, ranks * CHUNK), jnp.bfloat16),
            pltpu.VMEM((NP // 2, segs), jnp.float32),
            pltpu.VMEM((ranks, slows, segs), term),
            pltpu.VMEM((ranks, slows, segs), term),
            pltpu.SemaphoreType.DMA((2, chunks)),
            pltpu.SemaphoreType.DMA((2, chunks)),
            pltpu.SemaphoreType.DMA((2,)),
            pltpu.SemaphoreType.DMA((2,)),
            pltpu.SemaphoreType.DMA((chunks,)),
            pltpu.SemaphoreType.DMA((chunks,)),
            pltpu.SemaphoreType.DMA((chunks,)),
            pltpu.SemaphoreType.DMA((chunks,)),
            pltpu.SemaphoreType.DMA((chunks,)),
            pltpu.SemaphoreType.DMA((4,)),
        ],
        compiler_params=pltpu.CompilerParams(vmem_limit_bytes=VMEM_LIMIT, collective_id=0, has_side_effects=True),
        cost_estimate=pl.CostEstimate(flops=7 << 30, bytes_accessed=8 << 20, transcendentals=0),
        name="beamform",
    )(*[pltpu.with_memory_space_constraint(x, pltpu.HBM) for x in (offsets, signal, mask, table, slow)])


def store_kernel(beam_ref, power_ref, beam_out, power_out, sems):
    bins = beam_ref.shape[0]

    def copy(f):
        return pltpu.make_async_copy(beam_ref.at[f], beam_out.at[f], sems.at[f])

    last = pltpu.make_async_copy(power_ref, power_out, sems.at[bins])
    for f in range(bins):
        copy(f).start()
    last.start()
    for f in range(bins):
        copy(f).wait()
    last.wait()


def store(beam, power):
    vmem, anywhere = pl.BlockSpec(memory_space=pltpu.VMEM), pl.BlockSpec(memory_space=pl.ANY)
    return pl.pallas_call(
        store_kernel,
        out_shape=(jax.ShapeDtypeStruct(beam.shape, beam.dtype), jax.ShapeDtypeStruct(power.shape, power.dtype)),
        in_specs=[vmem, vmem],
        out_specs=(anywhere, anywhere),
        scratch_shapes=[pltpu.SemaphoreType.DMA((beam.shape[0] + 1,))],
        cost_estimate=pl.CostEstimate(flops=0, bytes_accessed=2 * beam.size * 4, transcendentals=0),
        compiler_params=pltpu.CompilerParams(vmem_limit_bytes=8 << 20),
        name="store",
    )(*[pltpu.with_memory_space_constraint(x, pltpu.VMEM) for x in (beam, power)])


def local(signal, channel_mask, seg_offsets, slow_steps):
    ranks, blocks = lax.axis_size("chan"), lax.axis_size("tm")
    return store(*fused(signal, channel_mask[None, :], seg_offsets, make_table(), slow_steps[None, :], ranks, blocks))


def solution(mesh):
    in_specs = (P("chan", "tm"), P("chan"), P("tm"), P())
    out_specs = (P("chan", None, None, "tm"), P("chan", "tm"))
    return jax.shard_map(local, mesh=mesh, in_specs=in_specs, out_specs=out_specs, check_vma=False)
```

```python
import functools
import math

import jax
import jax.numpy as jnp
import ml_dtypes
import numpy as np
from jax import lax
from jax.experimental import pallas as pl
from jax.experimental.pallas import tpu as pltpu
from jax.sharding import PartitionSpec as P

SEG = 256
NF = 128
NP = 512
SUBSTEPS = 16
HOP = 64
LANES = 128
CHUNK = 16
ROWS = 64
PAD = 8
VMEM_LIMIT = 46 * 1024 * 1024


def make_table():
    points = np.arange(SEG)
    bins = np.arange(1, NF + 1)
    taper = 0.5 - 0.5 * np.cos(2.0 * np.pi * points / SEG)
    angle = ((bins[:, None] * points[None, :]) % SEG) * (2.0 * np.pi / SEG)
    scale = 1.0 / math.sqrt(3.0 * SEG / 8.0)
    table = np.stack([taper * np.cos(angle), -taper * np.sin(angle)]).reshape(2, 2, NF // 2, SEG) * scale
    table = table.transpose(1, 0, 2, 3).reshape(2 * NF, SEG)
    return jnp.asarray(table.astype(np.float32).astype(ml_dtypes.bfloat16))


def turn(index):
    quarter = SEG * SUBSTEPS // 4
    quadrant = (index + quarter // 2) >> 10
    x = (index - quadrant * quarter).astype(jnp.float32) * (0.5 * math.pi / quarter)
    y = x * x
    sin = x * (1.0 + y * (-1.0 / 6 + y * (1.0 / 120 + y * (-1.0 / 5040 + y * (1.0 / 362880)))))
    cos = 1.0 + y * (-0.5 + y * (1.0 / 24 + y * (-1.0 / 720 + y * (1.0 / 40320))))
    odd = (quadrant & 1) == 1
    c, d = jnp.where(odd, sin, cos), jnp.where(odd, cos, sin)
    return jnp.where(((quadrant + 1) & 2) == 2, -c, c), jnp.where((quadrant & 2) == 2, -d, d)


def fused_kernel(offsets_ref, signal_ref, channel_mask_ref, taper_ref, steps_ref, beam_ref, power_ref, offs, mask_ref, table_ref, slow_ref, x_ref, slow, held_signal, p0, p1, s0, s1, send, recv, steer, energy, terms, arrived, send_sems, recv_sems, power_sems, halo_sems, signal_sends, signal_recvs, edge_sends, edge_recvs, load_sems, small_sems, *, ranks, blocks):
    chans = signal_ref.shape[0]
    chunks = chans // CHUNK
    step = p0.shape[0] // CHUNK
    segs = step - PAD
    own = NF // ranks
    slows = NP // ranks
    width = ranks * CHUNK
    total = chans * ranks
    modulus = SEG * SUBSTEPS
    me = lax.axis_index("chan")

    tm = lax.axis_index("tm")
    half = ranks // 2
    side = me // half
    mirror = (1 - side) * half + lax.rem(me, half)
    span = signal_ref.shape[1]
    half_bins = NF // 2

    def peer(d):
        return (1 - side + d // half) % 2 * half + ((me % half) ^ (d % half))

    barrier = pltpu.get_barrier_semaphore()
    mesh_ids = pl.DeviceIdType.MESH

    def greet(d, carry):
        pl.semaphore_signal(barrier, inc=1, device_id={"chan": peer(d)}, device_id_type=mesh_ids)
        return carry

    def others_of(body):
        lax.fori_loop(0, half, body, 0, unroll=8)
        lax.fori_loop(half + 1, ranks, body, 0, unroll=min(7, half - 1))

    @pl.when(tm > 0)
    def _():
        pl.semaphore_signal(barrier, inc=1, device_id={"tm": tm - 1}, device_id_type=mesh_ids)

    @pl.when(tm < blocks - 1)
    def _():
        pl.semaphore_signal(barrier, inc=1, device_id={"tm": tm + 1}, device_id_type=mesh_ids)

    others_of(greet)

    smalls = ((channel_mask_ref, mask_ref), (taper_ref, table_ref), (offsets_ref, offs), (steps_ref, slow_ref))
    load_mask, load_table, load_offsets, load_steps = [pltpu.make_async_copy(*pair, small_sems.at[i]) for i, pair in enumerate(smalls)]
    load_mask.start()
    for chunk in range(chunks):
        rows = pl.ds(chunk * CHUNK, CHUNK)
        pltpu.make_async_copy(signal_ref.at[rows], x_ref.at[rows], load_sems.at[chunk]).start()

    load_table.start()
    load_offsets.start()
    load_steps.start()

    def load(chunk):
        rows = pl.ds(pl.multiple_of(chunk * CHUNK, CHUNK), CHUNK)
        return pltpu.make_async_copy(signal_ref.at[rows], x_ref.at[rows], load_sems.at[chunk])

    edge = SEG // LANES

    def mask_tiles(chunk, low, high):
        rows = pl.ds(pl.multiple_of(chunk * CHUNK, CHUNK), CHUNK)
        across = lax.broadcasted_iota(jnp.int32, (CHUNK, chans), 1)
        down = lax.broadcasted_iota(jnp.int32, (CHUNK, chans), 0) + chunk * CHUNK
        live = jnp.broadcast_to(mask_ref[...].astype(jnp.float32), (CHUNK, chans))
        mask = jnp.sum(jnp.where(across == down, live, 0.0), axis=1, keepdims=True)
        mask = jnp.broadcast_to(mask, (CHUNK, LANES)).astype(jnp.bfloat16)

        def one(tile, carry):
            columns = pl.ds(pl.multiple_of(tile * LANES, LANES), LANES)
            held_signal[0, rows, columns] = x_ref[rows, columns] * mask
            return carry

        lax.fori_loop(low, high, one, 0, unroll=(high - low) // 2)

    def mask_edge(chunk, carry):
        load(chunk).wait()
        mask_tiles(chunk, 0, edge)
        return carry

    def mask_rows(chunk, carry):
        mask_tiles(chunk, edge, span // LANES)
        return carry

    load_mask.wait()
    lax.fori_loop(0, chunks, mask_edge, 0)
    lax.fori_loop(0, 3, mask_rows, 0)
    pl.semaphore_wait(barrier, ranks - 1 + jnp.where(tm > 0, 1, 0) + jnp.where(tm < blocks - 1, 1, 0))

    def halo_copy(to):
        return pltpu.make_async_remote_copy(
            src_ref=held_signal.at[0, :, pl.ds(0, SEG)],
            dst_ref=held_signal.at[0, :, pl.ds(span, SEG)],
            send_sem=halo_sems.at[0],
            recv_sem=halo_sems.at[1],
            device_id={"tm": to},
            device_id_type=mesh_ids,
        )

    def signal_copy(chunk):
        rows = pl.ds(pl.multiple_of(chunk * CHUNK, CHUNK), CHUNK)
        return pltpu.make_async_remote_copy(
            src_ref=held_signal.at[0, rows, pl.ds(0, span)],
            dst_ref=held_signal.at[1, rows, pl.ds(0, span)],
            send_sem=signal_sends.at[chunk],
            recv_sem=signal_recvs.at[chunk],
            device_id={"chan": mirror},
            device_id_type=mesh_ids,
        )

    def edge_copy(chunk, to):
        rows = pl.ds(pl.multiple_of(chunk * CHUNK, CHUNK), CHUNK)
        return pltpu.make_async_remote_copy(
            src_ref=held_signal.at[1, rows, pl.ds(0, SEG)],
            dst_ref=held_signal.at[1, rows, pl.ds(span, SEG)],
            send_sem=edge_sends.at[chunk],
            recv_sem=edge_recvs.at[chunk],
            device_id={"tm": to},
            device_id_type=mesh_ids,
        )

    def send_signal(chunk, carry):
        signal_copy(chunk).start()
        return carry

    @pl.when(tm > 0)
    def _():
        halo_copy(tm - 1).start()

    lax.fori_loop(0, 3, send_signal, 0)
    lax.fori_loop(3, chunks, mask_rows, 0)

    @pl.when(tm == blocks - 1)
    def _():
        held_signal[:, :, span:] = jnp.zeros((2, chans, SEG), jnp.bfloat16)

    def block_copy(slot, chunk, origin, to):
        return pltpu.make_async_remote_copy(
            src_ref=send.at[slot, chunk, pl.ds(lax.rem(to, half) * own, own)],
            dst_ref=recv.at[chunk, origin],
            send_sem=send_sems.at[slot, chunk],
            recv_sem=recv_sems.at[slot, chunk],
            device_id={"chan": to},
            device_id_type=mesh_ids,
        )

    inner = 2 * ((span - 3 * LANES) // LANES + 1)

    def spectra(slot, chunk, origin, edge_ready):
        top = pl.multiple_of(chunk * CHUNK, CHUNK)

        def gather(s, carry):
            start = pl.multiple_of((s // 2) * LANES, LANES)
            back = LANES - (offs[s] - start)
            tiles = held_signal[slot, pl.ds(top, CHUNK), pl.ds(start, 3 * LANES)].astype(jnp.float32)
            a, b, c = [pltpu.roll(tiles[:, i * LANES:(i + 1) * LANES], back, 1) for i in range(3)]
            keep = lax.broadcasted_iota(jnp.int32, (CHUNK, LANES), 1) < back
            p0[pl.ds(s, CHUNK, stride=step), :] = jnp.where(keep, a, b)
            p1[pl.ds(s, CHUNK, stride=step), :] = jnp.where(keep, b, c)
            return carry

        lax.fori_loop(0, inner, gather, 0, unroll=124)
        edge_ready()
        lax.fori_loop(inner, segs, gather, 0, unroll=4)
        table = table_ref[pl.ds(pl.multiple_of(side * NF, NF), NF), :]

        def transform(i, carry):
            pair = [pl.ds(pl.multiple_of((2 * i + part) * step, 8), segs) for part in range(2)]
            piece = jnp.concatenate([jnp.concatenate([p0[rows, :], p1[rows, :]], axis=1) for rows in pair]).astype(jnp.bfloat16)
            spec = lax.dot_general(table, piece, (((1,), (1,)), ((), ())), preferred_element_type=jnp.float32)
            for part in range(2):
                both = spec[:, part * segs:(part + 1) * segs]
                s0[pl.ds(2 * i + part, half_bins, stride=CHUNK + 8), :] = both[:half_bins]
                s1[pl.ds(2 * i + part, half_bins, stride=CHUNK + 8), :] = both[half_bins:]
            return carry

        lax.fori_loop(0, CHUNK // 2, transform, 0, unroll=8)

        def pack(f, carry):
            rows = pl.ds(pl.multiple_of(f * (CHUNK + 8), 8), CHUNK)
            send[slot, chunk, f] = jnp.concatenate([s0[rows, :], s1[rows, :]], axis=1).astype(jnp.bfloat16)
            return carry

        lax.fori_loop(0, half_bins, pack, 0, unroll=8)

        def launch(d, carry):
            block_copy(slot, chunk, origin, peer(ranks + half - d)).start()
            return carry

        lax.fori_loop(half + 1, ranks, launch, 0)
        recv[chunk, origin] = send[slot, chunk, pl.ds(lax.rem(me, half) * own, own)]

    load_table.wait()
    load_offsets.wait()
    load_steps.wait()

    def own_spectra(chunk, carry):
        def edge_ready():
            @pl.when((chunk == 0) & (tm < blocks - 1))
            def _():
                halo_copy(tm + 1).wait_recv()

        spectra(0, chunk, me, edge_ready)
        return carry

    lax.fori_loop(0, chunks, own_spectra, 0)

    for block in range(NP // LANES):
        row = slow_ref[:, block * LANES:(block + 1) * LANES].astype(jnp.float32)
        across = lax.broadcasted_iota(jnp.int32, (LANES, LANES), 1)
        down = lax.broadcasted_iota(jnp.int32, (LANES, LANES), 0)
        column = jnp.sum(jnp.where(across == down, jnp.broadcast_to(row, (LANES, LANES)), 0.0), axis=1, keepdims=True)
        slow[block * LANES:(block + 1) * LANES, :] = jnp.broadcast_to(column, (LANES, LANES)).astype(jnp.int32)

    def steering(step, carry):
        f, rows = step // (NP // ROWS), lax.rem(step, NP // ROWS) * ROWS
        rows = pl.multiple_of(rows, ROWS)
        kp = (slow[pl.ds(rows, ROWS), :] * (me * own + f + 1)) & (modulus - 1)
        lane = lax.broadcasted_iota(jnp.int32, (ROWS, LANES), 1)
        first = (lane // CHUNK) * chans + (lane & (CHUNK - 1))
        scale = 1.0 / math.sqrt(total)
        cos0, sin0 = turn((kp * first) & (modulus - 1))
        cos0, sin0 = cos0 * scale, sin0 * scale
        hops = jnp.where(lane == 0, CHUNK, (LANES // CHUNK) * chans)
        cosp, sinp = turn((kp * hops) & (modulus - 1))
        rc, rs, bc, bs = [jnp.broadcast_to(v[:, i:i + 1], (ROWS, LANES)) for i in (0, 1) for v in (cosp, sinp)]
        for block in range(width // LANES):
            columns = slice(block * LANES, (block + 1) * LANES)
            cos, sin = cos0, sin0
            for chunk in range(chunks):
                steer[f, chunk, pl.ds(rows, ROWS), columns] = cos.astype(jnp.bfloat16)
                steer[f, chunk, pl.ds(NP + rows, ROWS), columns] = sin.astype(jnp.bfloat16)
                cos, sin = cos * rc - sin * rs, cos * rs + sin * rc
            cos0, sin0 = cos0 * bc - sin0 * bs, cos0 * bs + sin0 * bc
        return carry

    steps = own * (NP // ROWS)

    def mirror_spectra(chunk, carry):
        lax.fori_loop(steps * chunk // (2 * chunks), steps * (chunk + 1) // (2 * chunks), steering, 0)
        signal_copy(chunk).wait_send()

        @pl.when(chunk + 3 < chunks)
        def _():
            signal_copy(chunk + 3).start()

        signal_copy(chunk).wait_recv()

        @pl.when(tm > 0)
        def _():
            edge_copy(chunk, tm - 1).start()

        def edge_ready():
            @pl.when(tm < blocks - 1)
            def _():
                edge_copy(chunk, tm + 1).wait_recv()

        spectra(1, chunk, mirror, edge_ready)
        return carry

    lax.fori_loop(0, chunks, mirror_spectra, 0)
    lax.fori_loop(steps // 2, steps, steering, 0)

    others = pl.ds(0, ranks - 1)

    def arrivals(slot, chunk):
        held = recv.at[chunk, pl.ds(0, half - 1)]
        pltpu.make_async_copy(held, held, recv_sems.at[slot, chunk]).wait()

    def add(chunk, first):
        arrivals(0, chunk)
        arrivals(1, chunk)

        def one_bin(f, carry):
            spec = recv[chunk, :, f].reshape(width, 2 * segs)
            both = jnp.dot(steer[f, chunk], spec, preferred_element_type=jnp.float32)
            real = both[:NP, :segs] - both[NP:, segs:]
            imag = both[:NP, segs:] + both[NP:, :segs]
            beam_ref[f, 0] = real if first else beam_ref[f, 0] + real
            beam_ref[f, 1] = imag if first else beam_ref[f, 1] + imag
            return carry

        lax.fori_loop(0, own, one_bin, 0, unroll=8)

    add(0, True)

    def more(chunk, carry):
        add(chunk, False)
        return carry

    lax.fori_loop(1, chunks - 1, more, 0)

    def power_copy(to):
        return pltpu.make_async_remote_copy(
            src_ref=terms.at[to],
            dst_ref=arrived.at[me],
            send_sem=power_sems.at[0],
            recv_sem=power_sems.at[1],
            device_id={"chan": to},
            device_id_type=pl.DeviceIdType.MESH,
        )

    last = chunks - 1
    rows_of_side = NP // 2
    energy[...] = jnp.zeros((rows_of_side, segs), jnp.float32)

    def half_sum(f, group, base, count):
        columns = pl.ds(pl.multiple_of(group * (width // 2), width // 2), width // 2)
        steps = [steer[f, last, pl.ds(base + part * NP, count), columns] for part in range(2)]
        spec = recv[last, pl.ds(group * half, half), f].reshape(width // 2, 2 * segs)
        turned = jnp.concatenate([-spec[:, segs:], spec[:, :segs]], axis=1)
        both = jnp.dot(jnp.concatenate(steps, axis=1), jnp.concatenate([spec, turned]), preferred_element_type=jnp.float32)
        return both[:, :segs], both[:, segs:]

    arrivals(0, last)

    def own_half(f, carry):
        real, imag = half_sum(f, side, 0, NP)
        beam_ref[f, 0] += real
        beam_ref[f, 1] += imag
        return carry

    lax.fori_loop(0, own, own_half, 0, unroll=8)
    arrivals(1, last)

    def finish_side(phase, carry):
        owners = lax.rem(side + 1 + phase, 2)
        base = pl.multiple_of(owners * rows_of_side, rows_of_side)
        rows = pl.ds(base, rows_of_side)

        def one_bin(f, acc):
            real, imag = half_sum(f, 1 - side, base, rows_of_side)
            real, imag = beam_ref[f, 0, rows, :] + real, beam_ref[f, 1, rows, :] + imag
            beam_ref[f, 0, rows, :] = real
            beam_ref[f, 1, rows, :] = imag
            energy[...] = jnp.where(f == 0, 0.0, energy[...]) + (real * real + imag * imag)
            return acc

        lax.fori_loop(0, own, one_bin, 0, unroll=8)
        mine = terms.at[pl.ds(owners * half, half)]
        mine[...] = (energy[...] * (1.0 / NF)).reshape(half, slows, segs).astype(terms.dtype)

        def power_term(d, carry):
            power_copy(peer(half - 1 - d + phase * (ranks + 1))).start()
            return carry

        lax.fori_loop(phase * (half + 1), half + phase * half, power_term, 0)
        return carry

    lax.fori_loop(0, 2, finish_side, 0)
    arrived[me] = terms[me]

    def finish(chunk, carry):
        sent = recv.at[chunk, pl.ds(0, half - 1)]
        pltpu.make_async_copy(sent, sent, send_sems.at[0, chunk]).wait()
        pltpu.make_async_copy(sent, sent, send_sems.at[1, chunk]).wait()

        @pl.when(tm > 0)
        def _():
            edge_copy(chunk, tm - 1).wait_send()

        return carry

    lax.fori_loop(0, chunks, finish, 0)

    @pl.when(tm > 0)
    def _():
        halo_copy(tm - 1).wait_send()

    pltpu.make_async_copy(arrived.at[others], arrived.at[others], power_sems.at[1]).wait()

    def sum_up(r, acc):
        return acc + arrived[r].astype(jnp.float32)

    power_ref[...] = lax.fori_loop(0, ranks, sum_up, jnp.zeros((slows, segs), jnp.float32), unroll=16)

    pltpu.make_async_copy(terms.at[others], terms.at[others], power_sems.at[0]).wait()


def fused(signal, mask, offsets, table, slow, ranks, blocks):
    chans, segs = signal.shape[0], offsets.shape[0]
    slows = NP // ranks
    term = jnp.bfloat16 if slows % 16 == 0 else jnp.float32
    own, chunks = NF // ranks, chans // CHUNK
    vmem = pl.BlockSpec(memory_space=pltpu.VMEM)
    return pl.pallas_call(
        functools.partial(fused_kernel, ranks=ranks, blocks=blocks),
        out_shape=(
            pltpu.VMEM((own, 2, NP, segs), jnp.float32),
            pltpu.VMEM((NP // ranks, segs), jnp.float32),
        ),
        in_specs=[pl.BlockSpec(memory_space=pl.ANY)] * 5,
        out_specs=(vmem, vmem),
        scratch_shapes=[
            pltpu.SMEM(offsets.shape, offsets.dtype),
            pltpu.VMEM(mask.shape, mask.dtype),
            pltpu.VMEM(table.shape, table.dtype),
            pltpu.VMEM(slow.shape, slow.dtype),
            pltpu.VMEM(signal.shape, signal.dtype),
            pltpu.VMEM((NP, LANES), jnp.int32),
            pltpu.VMEM((2, chans, signal.shape[1] + SEG), jnp.bfloat16),
        ]
        + [pltpu.VMEM((CHUNK * (segs + PAD), LANES), jnp.float32)] * 2
        + [pltpu.VMEM((NF // 2 * (CHUNK + 8), segs), jnp.float32)] * 2
        + [
            pltpu.VMEM((2, chunks, NF // 2, CHUNK, 2 * segs), jnp.bfloat16),
            pltpu.VMEM((chunks, ranks, own, CHUNK, 2 * segs), jnp.bfloat16),
            pltpu.VMEM((own, chunks, 2 * NP, ranks * CHUNK), jnp.bfloat16),
            pltpu.VMEM((NP // 2, segs), jnp.float32),
            pltpu.VMEM((ranks, slows, segs), term),
            pltpu.VMEM((ranks, slows, segs), term),
            pltpu.SemaphoreType.DMA((2, chunks)),
            pltpu.SemaphoreType.DMA((2, chunks)),
            pltpu.SemaphoreType.DMA((2,)),
            pltpu.SemaphoreType.DMA((2,)),
            pltpu.SemaphoreType.DMA((chunks,)),
            pltpu.SemaphoreType.DMA((chunks,)),
            pltpu.SemaphoreType.DMA((chunks,)),
            pltpu.SemaphoreType.DMA((chunks,)),
            pltpu.SemaphoreType.DMA((chunks,)),
            pltpu.SemaphoreType.DMA((4,)),
        ],
        compiler_params=pltpu.CompilerParams(vmem_limit_bytes=VMEM_LIMIT, collective_id=0, has_side_effects=True),
        cost_estimate=pl.CostEstimate(flops=7 << 30, bytes_accessed=8 << 20, transcendentals=0),
        name="beamform",
    )(*[pltpu.with_memory_space_constraint(x, pltpu.HBM) for x in (offsets, signal, mask, table, slow)])


def store_kernel(beam_ref, power_ref, beam_out, power_out, sems):
    bins = beam_ref.shape[0]

    def copy(f):
        return pltpu.make_async_copy(beam_ref.at[f], beam_out.at[f], sems.at[f])

    last = pltpu.make_async_copy(power_ref, power_out, sems.at[bins])
    for f in range(bins):
        copy(f).start()
    last.start()
    for f in range(bins):
        copy(f).wait()
    last.wait()


def store(beam, power):
    vmem, anywhere = pl.BlockSpec(memory_space=pltpu.VMEM), pl.BlockSpec(memory_space=pl.ANY)
    return pl.pallas_call(
        store_kernel,
        out_shape=(jax.ShapeDtypeStruct(beam.shape, beam.dtype), jax.ShapeDtypeStruct(power.shape, power.dtype)),
        in_specs=[vmem, vmem],
        out_specs=(anywhere, anywhere),
        scratch_shapes=[pltpu.SemaphoreType.DMA((beam.shape[0] + 1,))],
        cost_estimate=pl.CostEstimate(flops=0, bytes_accessed=2 * beam.size * 4, transcendentals=0),
        compiler_params=pltpu.CompilerParams(vmem_limit_bytes=8 << 20),
        name="store",
    )(*[pltpu.with_memory_space_constraint(x, pltpu.VMEM) for x in (beam, power)])


def local(signal, channel_mask, seg_offsets, slow_steps):
    ranks, blocks = lax.axis_size("chan"), lax.axis_size("tm")
    return store(*fused(signal, channel_mask[None, :], seg_offsets, make_table(), slow_steps[None, :], ranks, blocks))


def solution(mesh):
    in_specs = (P("chan", "tm"), P("chan"), P("tm"), P())
    out_specs = (P("chan", None, None, "tm"), P("chan", "tm"))
    return jax.shard_map(local, mesh=mesh, in_specs=in_specs, out_specs=out_specs, check_vma=False)
```
